32 devices in a mesh: ctx: 8 (over z, x), batch: 4 (over y, core).
Axes of the slice: x: 2, y: 2, z: 4, core: 2. Of those that a mesh axis runs over, the one named last changes fastest.
Arguments:
- kda_query: bfloat16 [4096, 2048], P(('batch', 'ctx')), parts along dimension 0, may hold values from -6 to 6
- kda_key: bfloat16 [4096, 2048], P(('batch', 'ctx')), parts along dimension 0, may hold values from -6 to 6
- kda_value: bfloat16 [4096, 2048], P(('batch', 'ctx')), parts along dimension 0, may hold values from -6 to 6
- log_decay: bfloat16 [4096, 2048], P(('batch', 'ctx')), parts along dimension 0, may hold values from -2 to 0
- write_rate: float32 [4096, 16], P(('batch', 'ctx')), parts along dimension 0, may hold values from 0.01 to 0.9
- mla_query: bfloat16 [4096, 3072], P(('batch', 'ctx')), parts along dimension 0, may hold values from -8 to 8
- latents: bfloat16 [4096, 576], P(('batch', 'ctx')), parts along dimension 0, may hold values from -8 to 8
- key_up: bfloat16 [512, 2048], replicated, may hold values from -0.25 to 0.25
- value_up: bfloat16 [512, 2048], replicated, may hold values from -0.25 to 0.25
- doc_lengths: int32 [32], P('batch'), parts along dimension 0, may hold values from 1 to 512, 1024 in all
Outputs:
- kda_out: bfloat16 [4096, 2048], P(('batch', 'ctx')), parts along dimension 0
- mla_out: bfloat16 [4096, 2048], P(('batch', 'ctx')), parts along dimension 0
The draws below stay inside these ranges and needn't reach their ends.
There are 4 independent parts, one for each index of `batch`. The reference program is written for one: setup_inputs(seed, part) draws one part's arguments, and reference() takes and returns one part's arrays. A program takes and returns all parts, laid end to end along the dimension named above; an argument that names none is the same for every part. Nothing has to cross between parts.
Inputs may be any that keep to these rules, and one draw needn't show every extreme that they name: `doc_lengths`: 8 lengths of the documents of one context in order; they sum to 1024 and the longest is exactly 512.
All inputs are finite; a program needn't handle non-finite values.
Results may differ from the reference program's by a relative error of at most 0.009.
Values may be sent and summed in bfloat16 or wider, within the bound.
No kernel may reach another device: no remote copies, remote signals or barrier semaphores. Data moves between devices by JAX's collectives and lax.ppermute only.
A program may use at most 192 MiB of HBM per device.

```python
import math
import jax
import jax.numpy as jnp
import numpy as np
from jax import lax

HEADS = 16
DK = 128
DV = 128
NOPE = 128
ROPE = 64
LATENT = 512
BLOCK = 64
NDOCS = 8
TOK_DEV = 128
CONTEXT_SIZE = 1024


def loguniform_draw(key, shape_all, lowest, highest):
    return jnp.exp(jax.random.uniform(key, shape_all, jnp.float32, jnp.log(lowest), jnp.log(highest)))


def draw_latents(key, part):
    shape_all = (CONTEXT_SIZE, LATENT + ROPE)
    base = jnp.clip(jax.random.normal(jax.random.fold_in(key, 1), shape_all, jnp.float32), -6.0, 6.0)
    return base.astype(jnp.bfloat16)


def draw_mla_query(key, part):
    shape_all = (CONTEXT_SIZE, HEADS, NOPE + ROPE)
    base = jnp.clip(jax.random.normal(jax.random.fold_in(key, 3), shape_all, jnp.float32), -6.0, 6.0)
    return base.reshape(CONTEXT_SIZE, HEADS * (NOPE + ROPE)).astype(jnp.bfloat16)


def draw_log_decay(key, part):
    head_bits = jax.random.bernoulli(jax.random.fold_in(key, 21), 0.5, (HEADS, 1))
    slow_rate = loguniform_draw(jax.random.fold_in(key, 22), (HEADS, DK), 0.1 / CONTEXT_SIZE, 1.0 / CONTEXT_SIZE)
    fast_rate = loguniform_draw(jax.random.fold_in(key, 23), (HEADS, DK), 1.0 / CONTEXT_SIZE, 1.0 / 25.0)
    channel_decay_rate = jnp.where(head_bits, slow_rate, fast_rate)
    approximate = jax.random.uniform(jax.random.fold_in(key, 25), (CONTEXT_SIZE, HEADS, DK), jnp.float32, 0.5, 1.5)
    segment_factor = loguniform_draw(jax.random.fold_in(key, 26), (CONTEXT_SIZE // TOK_DEV, 1, 1), 0.5, 2.0)
    segment_factor = jnp.repeat(segment_factor, TOK_DEV, axis=0)
    spike_positions = jax.random.randint(jax.random.fold_in(key, 27), (6,), 0, CONTEXT_SIZE)
    spike_lengths = jnp.log(jax.random.uniform(jax.random.fold_in(key, 28), (6,), jnp.float32, 0.5, 0.8))
    match_count = (jnp.arange(CONTEXT_SIZE)[:, None] == spike_positions[None, :]).astype(jnp.float32)
    spike_run = jnp.sum(match_count * spike_lengths[None, :], axis=1)
    logarithm_decay = -channel_decay_rate[None] * approximate * segment_factor + spike_run[:, None, None]
    return logarithm_decay.reshape(CONTEXT_SIZE, HEADS * DK).astype(jnp.bfloat16)


def draw_write_rate(key, part):
    head_base = loguniform_draw(jax.random.fold_in(key, 31), (1, HEADS), 0.02, 0.6)
    approximate = jax.random.uniform(jax.random.fold_in(key, 32), (CONTEXT_SIZE, HEADS), jnp.float32, 0.5, 1.5)
    return (head_base * approximate).astype(jnp.float32)


def level_of(stream_key, dims, cuts, smallest, high):
    loudness = 1.0
    for dim, parts in cuts:
        heights = jax.random.uniform(jax.random.fold_in(jax.random.fold_in(stream_key, 6), dim), (parts,), jnp.float32, smallest / len(cuts), high / len(cuts))
        loudness = loudness * jnp.repeat(jnp.exp(heights), dims[dim] // parts).reshape((-1,) + (1,) * (len(dims) - 1 - dim))
    return loudness


def length_profile(amount, total, limit, lean):
    weights = [(1 << 20) // math.isqrt(rank ** lean) + 1 for rank in range(2, amount + 1)]
    spare, counts = total - limit - (amount - 1), [1] * (amount - 1)
    while spare > 0:
        candidates = [i for i in range(amount - 1) if counts[i] < limit]
        mass, remaining = sum([weights[i] for i in candidates]), spare
        for i in candidates:
            more = min(limit - counts[i], max(1, remaining * weights[i] // mass), spare)
            counts[i] = counts[i] + more
            spare = spare - more
    return np.array([limit] + counts)


def ragged(key, number_of, total, bound, lean):
    if number_of == 2:
        one = jax.random.randint(key, (), max(1, total - bound), min(bound, total - 1) + 1)
        return jnp.stack([one, total - one])
    tallies = jnp.asarray(length_profile(number_of, total, bound, lean), jnp.int32)
    couples = (number_of - 1) // 2
    source_of, receiver = tallies[1:1 + 2 * couples:2], tallies[2:2 + 2 * couples:2]
    room = jnp.minimum(source_of - 1, bound - receiver)
    shifted = jax.random.randint(jax.random.fold_in(key, 1), (couples,), 0, 1 << 20) % (room + 1)
    tallies = tallies.at[1:1 + 2 * couples:2].set(source_of - shifted).at[2:2 + 2 * couples:2].set(receiver + shifted)
    return tallies[jax.random.permutation(jax.random.fold_in(key, 2), number_of)]


def normal_values(rng, shape, scale, reach, split=(), kind=jnp.bfloat16):
    array = jax.random.normal(rng, shape, jnp.float32) * scale
    if len(split) > 0:
        array = level_of(rng, shape, split, -0.22, 0.18) * array
    return jnp.clip(array, min=-reach, max=reach).astype(kind)


def setup_inputs(seed: int = 0, part: int = 0) -> dict:
    splits = jax.random.split(jax.random.key(seed), 11)
    part_splits = jax.random.split(jax.random.fold_in(splits[10], part), 11)
    kda_query = normal_values(part_splits[0], (CONTEXT_SIZE, HEADS * DK), 1.0, 6.0, ((0, 8),))
    kda_key = normal_values(part_splits[1], (CONTEXT_SIZE, HEADS * DK), 1.0, 6.0, ((0, 8),))
    kda_value = normal_values(part_splits[2], (CONTEXT_SIZE, HEADS * DV), 1.0, 6.0, ((0, 8),))
    log_decay = draw_log_decay(jax.random.fold_in(jax.random.fold_in(splits[10], part), 71), part)
    write_rate = draw_write_rate(jax.random.fold_in(jax.random.fold_in(splits[10], part), 71), part)
    mla_query = draw_mla_query(jax.random.fold_in(jax.random.fold_in(splits[10], part), 71), part)
    latents = draw_latents(jax.random.fold_in(jax.random.fold_in(splits[10], part), 71), part)
    key_up = normal_values(splits[7], (LATENT, HEADS * NOPE), LATENT ** -0.5, 0.25)
    value_up = normal_values(splits[8], (LATENT, HEADS * DV), LATENT ** -0.5, 0.25)
    doc_lengths = ragged(part_splits[9], NDOCS, CONTEXT_SIZE, CONTEXT_SIZE // 2, 2).astype(jnp.int32)
    return {"kda_query": kda_query, "kda_key": kda_key, "kda_value": kda_value, "log_decay": log_decay, "write_rate": write_rate, "mla_query": mla_query, "latents": latents, "key_up": key_up, "value_up": value_up, "doc_lengths": doc_lengths}


PRECISE_PRODUCT = lax.Precision.HIGHEST

def unit_rows(values):
    return values * lax.rsqrt(lax.optimization_barrier(jnp.sum(values * values, axis=-1, keepdims=True)) + 1e-06)

def doc_of(positions, doc_starts):
    match_count = (doc_starts[None, :] <= positions[:, None]).astype(jnp.int32)
    return (lax.optimization_barrier(jnp.sum(match_count, axis=1)) - 1).astype(jnp.int32)

def unit_lower_inverse(strictly_lower):
    length = strictly_lower.shape[-1]
    identity = jnp.eye(length, dtype=jnp.float32)[None]
    result = identity - strictly_lower
    power_term = strictly_lower
    for level_index in range(length.bit_length() - 2):
        power_term = jnp.einsum('hij,hjk->hik', power_term, power_term, precision=PRECISE_PRODUCT)
        result = jnp.einsum('hij,hjk->hik', result, identity + power_term, precision=PRECISE_PRODUCT)
    return result

def block_terms(query_unit, keyvec, valvec, logarithm_decay, write_gain, docids, prevdoc):
    length = docids.shape[0]
    cumulative = jnp.cumsum(logarithm_decay, axis=0)
    growth = jnp.exp(cumulative)
    key_plus = keyvec * growth
    key_minus = keyvec * jnp.exp(-cumulative)
    query_plus = query_unit * growth
    places = jnp.arange(length)
    same_doc = docids[:, None] == docids[None, :]
    strict = (places[:, None] > places[None, :]) & same_doc
    causal = (places[:, None] >= places[None, :]) & same_doc
    follow = (docids == prevdoc).astype(jnp.float32)
    inner_prod = jnp.einsum('thk,shk->hts', key_plus, key_minus, precision=PRECISE_PRODUCT)
    strictly_lower = jnp.where(strict[None], inner_prod, 0.0) * jnp.transpose(write_gain)[:, :, None]
    inverse = unit_lower_inverse(strictly_lower)
    value_rhs = jnp.transpose(valvec * write_gain[:, :, None], (1, 0, 2))
    key_rhs = jnp.transpose(key_plus * (write_gain * follow[:, None])[:, :, None], (1, 0, 2))
    value_solution = jnp.einsum('hts,hsv->htv', inverse, value_rhs, precision=PRECISE_PRODUCT)
    solved_key = jnp.einsum('hts,hsk->htk', inverse, key_rhs, precision=PRECISE_PRODUCT)
    mixing = jnp.where(causal[None], jnp.einsum('thk,shk->hts', query_plus, key_minus, precision=PRECISE_PRODUCT), 0.0)
    local_output = jnp.einsum('hts,hsv->htv', mixing, value_solution, precision=PRECISE_PRODUCT)
    query_effective = jnp.transpose(query_plus * follow[:, None, None], (1, 0, 2)) - jnp.einsum('hts,hsk->htk', mixing, solved_key, precision=PRECISE_PRODUCT)
    last_doc = (docids == docids[length - 1]).astype(jnp.float32)
    key_trailing = keyvec * jnp.exp(cumulative[length - 1][None] - cumulative) * last_doc[:, None, None]
    growth_last = growth[length - 1]
    diagonal_map = growth_last[:, :, None] * jnp.eye(keyvec.shape[2], dtype=jnp.float32)[None]
    handed_operator = follow[length - 1] * diagonal_map - jnp.einsum('shk,hsj->hkj', key_trailing, solved_key, precision=PRECISE_PRODUCT)
    handed_update = jnp.einsum('omt,mor->mtr', key_trailing, value_solution, precision=PRECISE_PRODUCT)
    return (local_output, query_effective, handed_operator, handed_update)

def kda_layer(kda_query, kda_key, kda_value, log_decay, write_rate, docids):
    total_rows = kda_query.shape[0]
    head_count = write_rate.shape[1]
    query_unit = unit_rows(kda_query.astype(jnp.float32).reshape(total_rows, head_count, -1))
    keyvec = unit_rows(kda_key.astype(jnp.float32).reshape(total_rows, head_count, -1))
    valvec = kda_value.astype(jnp.float32).reshape(total_rows, head_count, -1)
    logarithm_decay = log_decay.astype(jnp.float32).reshape(total_rows, head_count, -1)
    blocks = total_rows // BLOCK
    prevdocs = jnp.concatenate([jnp.full((1,), -1, jnp.int32), docids[:-1]])[::BLOCK]

    def shaped(values):
        return values.reshape((blocks, BLOCK) + values.shape[1:])

    def advance(handed_forward, inputs):
        local_output, query_effective, handed_operator, handed_update = block_terms(*inputs)
        final_output = local_output + jnp.einsum('cor,crm->com', query_effective, handed_forward, precision=PRECISE_PRODUCT)
        handed_forward = jnp.einsum('ytn,yne->yte', handed_operator, handed_forward, precision=PRECISE_PRODUCT) + handed_update
        return (handed_forward, final_output)
    initial = jnp.zeros((head_count, keyvec.shape[2], valvec.shape[2]), jnp.float32)
    xs_all = (shaped(query_unit), shaped(keyvec), shaped(valvec), shaped(logarithm_decay), shaped(write_rate.astype(jnp.float32)), shaped(docids), prevdocs)
    _, outputs = lax.scan(advance, initial, xs_all)
    return jnp.transpose(outputs, (0, 2, 1, 3)).reshape(total_rows, -1).astype(jnp.bfloat16)

def mla_layer(mla_query, latents, key_up, value_up, docids):
    total_rows = latents.shape[0]
    head_count = key_up.shape[1] // NOPE
    latent_part = latents[:, :LATENT]
    keys_nope = jnp.dot(latent_part, key_up, preferred_element_type=jnp.float32).astype(jnp.bfloat16)
    values = jnp.dot(latent_part, value_up, preferred_element_type=jnp.float32).astype(jnp.bfloat16)
    keys_wide = keys_nope.astype(jnp.float32).reshape(total_rows, head_count, NOPE)
    values_wide = values.astype(jnp.float32).reshape(total_rows, head_count, -1)
    rope_keys = latents[:, LATENT:].astype(jnp.float32)
    queries = mla_query.astype(jnp.float32).reshape(total_rows, head_count, NOPE + ROPE)
    score_scale = 1.0 / math.sqrt(NOPE + ROPE)
    positions = jnp.arange(total_rows, dtype=jnp.int32)
    blocks = total_rows // TOK_DEV

    def attend(inputs):
        query_block, place_block, doc_block = inputs
        scores = jnp.einsum('thd,shd->hts', query_block[:, :, :NOPE], keys_wide)
        scores = (scores + jnp.einsum('thr,sr->hts', query_block[:, :, NOPE:], rope_keys)) * score_scale
        allowed = (positions[None, :] <= place_block[:, None]) & (docids[None, :] == doc_block[:, None])
        masked = jnp.where(allowed[None], scores, -1e+30)
        row_max = lax.optimization_barrier(jnp.max(masked, axis=2, keepdims=True))
        weights = jnp.where(allowed[None], jnp.exp(masked - row_max), 0.0)
        row_total = lax.optimization_barrier(jnp.sum(weights, axis=2))
        rounded = lax.optimization_barrier(weights.astype(jnp.bfloat16)).astype(jnp.float32)
        summed = jnp.einsum('hts,shv->thv', rounded, values_wide)
        return (summed / jnp.transpose(row_total)[:, :, None]).astype(jnp.bfloat16)
    outputs = lax.map(attend, (queries.reshape(blocks, TOK_DEV, head_count, NOPE + ROPE), positions.reshape(blocks, TOK_DEV), docids.reshape(blocks, TOK_DEV)))
    return outputs.reshape(total_rows, -1)

def reference(kda_query, kda_key, kda_value, log_decay, write_rate, mla_query, latents, key_up, value_up, doc_lengths):
    doc_starts = (jnp.cumsum(doc_lengths) - doc_lengths).astype(jnp.int32)
    positions = jnp.arange(latents.shape[0], dtype=jnp.int32)
    docids = doc_of(positions, doc_starts)
    kda_out = kda_layer(kda_query, kda_key, kda_value, log_decay, write_rate, docids)
    mla_out = mla_layer(mla_query, latents, key_up, value_up, docids)
    return (kda_out, mla_out)
```

```python
import functools
import math

import jax
import jax.numpy as jnp
import numpy as np
from jax import lax
from jax.experimental import pallas as pl
from jax.experimental.pallas import tpu as pltpu
from jax.sharding import PartitionSpec as P

NOPE = 128
ROPE = 64
LATENT = 512
GROUP = 4
VMEM = 32 * 1024 * 1024
BF = jnp.bfloat16
F32 = jnp.float32
NEG = -1e30


def mm(a, b):
    return jnp.dot(a, b, preferred_element_type=F32)


def mm_nt(a, b):
    return lax.dot_general(a, b, (((1,), (1,)), ((), ())), preferred_element_type=F32)


def mm_tn(a, b):
    return lax.dot_general(a, b, (((0,), (0,)), ((), ())), preferred_element_type=F32)


def doc_of(places, starts_ref, base, ndocs):
    total = jnp.zeros(jnp.shape(places), jnp.int32)
    for j in range(ndocs):
        total = total + (starts_ref[base + j] <= places).astype(jnp.int32)
    return total - 1


def kda_kernel(ndocs, sc, q_ref, k_ref, v_ref, g_ref, b_ref, mu_ref, qe_ref, lo_ref):
    rows = q_ref.shape[0]
    half = rows // 2
    heads = q_ref.shape[1] // 128
    group = sc[0] + pl.program_id(0)
    first = sc[1]
    ri = lax.broadcasted_iota(jnp.int32, (rows, rows), 0)
    ci = lax.broadcasted_iota(jnp.int32, (rows, rows), 1)
    doc_r = doc_of(first + ri, sc, 2, ndocs)
    doc_c = doc_of(first + ci, sc, 2, ndocs)
    prev = doc_of(first - 1, sc, 2, ndocs)
    last = doc_of(first + rows - 1, sc, 2, ndocs)
    same = doc_r == doc_c
    strict = same & (ri > ci)
    causal = same & (ri >= ci)
    follow = (doc_r == prev).astype(F32)
    tail = (doc_r == last).astype(F32)
    keep = (last == prev).astype(F32)
    eye = (ri == ci).astype(F32)
    tri = (ri >= ci).astype(BF)
    low = ci < half
    cum_all = mm(tri, g_ref[...])
    gains = b_ref[...]
    gain_lane = lax.broadcasted_iota(jnp.int32, gains.shape, 1)

    hs = range(heads)
    lhs, km, lhs_off, km_off, rhs, kt, qg, gl, gain = [], [], [], [], [], [], [], [], []
    for h in hs:
        cols = slice(h * 128, (h + 1) * 128)
        q = q_ref[:, cols].astype(F32)
        k = k_ref[:, cols].astype(F32)
        v = v_ref[:, cols].astype(F32)
        qn = q * lax.rsqrt(jnp.sum(q * q, axis=1, keepdims=True) + 1e-06)
        kn = k * lax.rsqrt(jnp.sum(k * k, axis=1, keepdims=True) + 1e-06)
        cum = cum_all[:, cols]
        b = jnp.sum(
            jnp.where(gain_lane == group * heads + h, gains, 0.0), axis=1, keepdims=True
        )
        quarter = half // 2
        m0 = cum[quarter - 1 : quarter]
        m1 = cum[half + quarter - 1 : half + quarter]
        mid = cum[half - 1 : half]
        end = cum[rows - 1 : rows]
        c0, c1 = cum[:half], cum[half:]
        dp = jnp.concatenate([jnp.exp(c0 - m0), jnp.exp(c1 - m1)], axis=0)
        dm = jnp.concatenate([jnp.exp(m0 - c0), jnp.exp(m1 - c1)], axis=0)
        op = jnp.exp(c1 - mid)
        om = jnp.exp(jnp.minimum(mid - cum, 0.0))
        growth = jnp.exp(cum)
        trail = jnp.exp(end - cum)
        lhs.append(jnp.concatenate([(kn * dp).astype(BF), (qn * dp).astype(BF)], axis=0))
        km.append((kn * dm).astype(BF))
        lhs_off.append(
            jnp.concatenate([(kn[half:] * op).astype(BF), (qn[half:] * op).astype(BF)], axis=0)
        )
        km_off.append((kn * om).astype(BF))
        rhs.append(
            jnp.concatenate([(kn * growth * (b * follow)).astype(BF), (v * b).astype(BF)], axis=1)
        )
        kt.append((kn * trail * tail).astype(BF))
        qg.append(qn * growth * follow)
        gl.append(jnp.exp(end) * keep)
        gain.append(b)

    a, mix = [], []
    for h in hs:
        p = mm_nt(lhs[h], km[h])
        o = mm_nt(lhs_off[h], km_off[h])
        pa, pq = p[:rows], p[rows:]
        pa = jnp.concatenate([pa[:half], jnp.where(low[half:], o[:half], pa[half:])], axis=0)
        pq = jnp.concatenate([pq[:half], jnp.where(low[half:], o[half:], pq[half:])], axis=0)
        a.append(jnp.where(strict, pa, 0.0) * gain[h])
        mix.append(jnp.where(causal, pq, 0.0).astype(BF))

    t = [eye - jnp.where((ri >> 1) == (ci >> 1), a[h], 0.0) for h in hs]
    shift = 1
    while (2 << shift) <= rows:
        level = ((ri >> (shift + 1)) == (ci >> (shift + 1))) & ((ri >> shift) != (ci >> shift))
        tb = [t[h].astype(BF) for h in hs]
        x = [mm(jnp.where(level, a[h], 0.0).astype(BF), tb[h]).astype(BF) for h in hs]
        t = [t[h] - mm(tb[h], x[h]) for h in hs]
        shift += 1

    wu = [mm(t[h].astype(BF), rhs[h]).astype(BF) for h in hs]
    for h in hs:
        cols = slice(h * 128, (h + 1) * 128)
        z = mm_tn(kt[h], wu[h])
        mu_ref[h, :, :128] = (eye * gl[h] - z[:, :128]).astype(BF)
        mu_ref[h, :, 128:] = z[:, 128:].astype(BF)
        y = mm(mix[h], wu[h])
        qe_ref[:, cols] = (qg[h] - y[:, :128]).astype(BF)
        lo_ref[:, cols] = y[:, 128:]


def kda_local(scalars, q, k, v, g, b, groups, ndocs):
    rows, width = q.shape[0], GROUP * 128
    heads = b.shape[1]
    wide = pl.BlockSpec((rows, width), lambda i, sc: (0, sc[0] + i))
    out_wide = pl.BlockSpec((rows, width), lambda i, sc: (0, i))
    return pl.pallas_call(
        functools.partial(kda_kernel, ndocs),
        grid_spec=pltpu.PrefetchScalarGridSpec(
            num_scalar_prefetch=1,
            grid=(groups,),
            in_specs=[wide, wide, wide, wide, pl.BlockSpec((rows, heads), lambda i, sc: (0, 0))],
            out_specs=[
                pl.BlockSpec((GROUP, 128, 256), lambda i, sc: (i, 0, 0)),
                out_wide,
                out_wide,
            ],
        ),
        out_shape=[
            jax.ShapeDtypeStruct((groups * GROUP, 128, 256), BF),
            jax.ShapeDtypeStruct((rows, groups * width), BF),
            jax.ShapeDtypeStruct((rows, groups * width), F32),
        ],
        compiler_params=pltpu.CompilerParams(vmem_limit_bytes=VMEM),
        cost_estimate=pl.CostEstimate(
            flops=groups * GROUP * 2 * 128**3 * 22,
            bytes_accessed=groups * width * rows * 16,
            transcendentals=0,
        ),
        name="kda_slab",
    )(scalars, q, k, v, g, b)


def pair_kernel(sc, own_ref, got_ref, pm_ref, pu_ref):
    def go(first_ref, second_ref):
        for h in range(own_ref.shape[0]):
            z = mm(second_ref[h, :, :128], first_ref[h])
            pm_ref[h] = z[:, :128].astype(BF)
            pu_ref[h] = (z[:, 128:] + second_ref[h, :, 128:].astype(F32)).astype(BF)

    @pl.when(sc[0] == 0)
    def _():
        go(own_ref, got_ref)

    @pl.when(sc[0] != 0)
    def _():
        go(got_ref, own_ref)


def arrived(sc, a_ref, b_ref, h):
    x = jnp.where(sc[2] == 1, a_ref[h].astype(F32), b_ref[h].astype(F32))
    return jnp.where(sc[1] == 1, 0.0, x).astype(BF)


def step_kernel(sc, pm_ref, pu_ref, a_ref, b_ref, out_ref):
    for h in range(pm_ref.shape[0]):
        x = arrived(sc, a_ref, b_ref, h)
        out_ref[h] = (mm(pm_ref[h], x) + pu_ref[h].astype(F32)).astype(BF)


def split_kernel(sc, own_ref, got_ref, a_ref, b_ref, mine_ref, send_ref):
    def go(mu_ref, plain_ref, moved_ref):
        for h in range(own_ref.shape[0]):
            x = arrived(sc, a_ref, b_ref, h)
            plain_ref[h] = x
            moved_ref[h] = (mm(mu_ref[h, :, :128], x) + mu_ref[h, :, 128:].astype(F32)).astype(BF)

    @pl.when(sc[0] == 0)
    def _():
        go(own_ref, mine_ref, send_ref)

    @pl.when(sc[0] != 0)
    def _():
        go(got_ref, send_ref, mine_ref)


def whole_call(kernel, name, scalars, args, outs):
    def full(shape):
        return pl.BlockSpec(shape, lambda i, sc, n=len(shape): (0,) * n)

    return pl.pallas_call(
        kernel,
        grid_spec=pltpu.PrefetchScalarGridSpec(
            num_scalar_prefetch=1,
            grid=(1,),
            in_specs=[full(x.shape) for x in args],
            out_specs=[full(o) for o in outs],
        ),
        out_shape=[jax.ShapeDtypeStruct(o, BF) for o in outs],
        compiler_params=pltpu.CompilerParams(vmem_limit_bytes=VMEM),
        name=name,
    )(scalars, *args)


def final_kernel(sc, qe_ref, lo_ref, s_ref, *rest):
    out_ref = rest[-1]
    for h in range(s_ref.shape[0]):
        cols = slice(h * 128, (h + 1) * 128)
        out_ref[:, cols] = (lo_ref[:, cols] + mm(qe_ref[:, cols], s_ref[h])).astype(BF)


def final(block, qe, lo, s, heads, previous):
    rows = qe.shape[0]
    half = s.shape[0]
    wide = pl.BlockSpec((rows, half * 128), lambda i, sc: (0, 0))
    args = [qe, lo, s]
    specs = [wide, wide, pl.BlockSpec(s.shape, lambda i, sc: (0, 0, 0))]
    aliases = {}
    if previous is not None:
        args.append(previous)
        specs.append(pl.BlockSpec(memory_space=pl.ANY))
        aliases = {4: 0}
    return pl.pallas_call(
        final_kernel,
        grid_spec=pltpu.PrefetchScalarGridSpec(
            num_scalar_prefetch=1,
            grid=(1,),
            in_specs=specs,
            out_specs=pl.BlockSpec((rows, half * 128), lambda i, sc: (0, sc[0])),
        ),
        out_shape=jax.ShapeDtypeStruct((rows, heads * 128), BF),
        input_output_aliases=aliases,
        compiler_params=pltpu.CompilerParams(vmem_limit_bytes=VMEM),
        name="kda_out",
    )(block, *args)


def mla_kernel(ndocs, n, window, has_previous, sc, *refs):
    q_ref, ku_ref, vu_ref = refs[:3]
    blocks = refs[3 : 3 + n]
    out_ref, lat_ref, bias_ref = refs[3 + n + int(has_previous) :]
    rows = q_ref.shape[0]
    keys = window * rows

    @pl.when(pl.program_id(0) == 0)
    def _():
        lat_ref[...] = jnp.zeros_like(lat_ref)
        for m in range(n):
            slot = sc[1 + m]

            @pl.when(slot >= 0)
            def _():
                lat_ref[pl.ds(pl.multiple_of(slot * rows, rows), rows), :] = blocks[m][...]

        here = sc[0] + lax.broadcasted_iota(jnp.int32, (rows, 1), 0)
        there = sc[0] - keys + rows + lax.broadcasted_iota(jnp.int32, (1, keys), 1)
        doc_q = doc_of(here, sc, 1 + n, ndocs)
        doc_k = doc_of(there, sc, 1 + n, ndocs)
        bias_ref[...] = jnp.where((there <= here) & (doc_q == doc_k), 0.0, NEG)

    factor = math.log2(math.e) / math.sqrt(NOPE + ROPE)
    lat = lat_ref[:, :LATENT]
    rope = lat_ref[:, LATENT:]
    kn = mm(lat, ku_ref[...]).astype(BF)
    vals = mm(lat, vu_ref[...]).astype(BF)
    bias = bias_ref[...]
    for h in range(out_ref.shape[1] // 128):
        cols = slice(h * 128, (h + 1) * 128)
        q = q_ref[:, h * (NOPE + ROPE) : (h + 1) * (NOPE + ROPE)]
        s = mm_nt(q, jnp.concatenate([kn[:, cols], rope], axis=1)) * factor + bias
        w = jnp.exp2(s - jnp.max(s, axis=1, keepdims=True))
        total = jnp.sum(w, axis=1, keepdims=True)
        out_ref[:, cols] = (mm(w.astype(BF), vals[:, cols]) / total).astype(BF)


def mla(scalars, q, ku, vu, blocks, window, ndocs, first, groups, previous):
    rows = q.shape[0]
    n = len(blocks)
    heads = ku.shape[1] // NOPE
    qw, w = GROUP * (NOPE + ROPE), GROUP * 128
    keys = window * rows
    args = [q, ku, vu, *blocks]
    specs = [
        pl.BlockSpec((rows, qw), lambda i, sc: (0, first + i)),
        pl.BlockSpec((LATENT, w), lambda i, sc: (0, first + i)),
        pl.BlockSpec((LATENT, w), lambda i, sc: (0, first + i)),
    ] + [pl.BlockSpec(x.shape, lambda i, sc: (0, 0)) for x in blocks]
    aliases = {}
    if previous is not None:
        args.append(previous)
        specs.append(pl.BlockSpec(memory_space=pl.ANY))
        aliases = {len(args): 0}
    return pl.pallas_call(
        functools.partial(mla_kernel, ndocs, n, window, previous is not None),
        grid_spec=pltpu.PrefetchScalarGridSpec(
            num_scalar_prefetch=1,
            grid=(groups,),
            in_specs=specs,
            out_specs=pl.BlockSpec((rows, w), lambda i, sc: (0, first + i)),
            scratch_shapes=[
                pltpu.VMEM((keys, LATENT + ROPE), BF),
                pltpu.VMEM((rows, keys), F32),
            ],
        ),
        out_shape=jax.ShapeDtypeStruct((rows, heads * 128), BF),
        input_output_aliases=aliases,
        compiler_params=pltpu.CompilerParams(vmem_limit_bytes=VMEM),
        cost_estimate=pl.CostEstimate(
            flops=2 * keys * groups * w * (2 * LATENT + 3 * rows),
            bytes_accessed=groups * w * 3000,
            transcendentals=0,
        ),
        name="mla_heads",
    )(scalars, *args)


def repaired(n, wanted):
    left = [i for i in range(n) if i not in wanted]
    out = dict(wanted)
    for a, b in zip(left[::2], left[1::2]):
        out[a], out[b] = b, a
    return [out[i] for i in range(n)]


def routes(n):
    reach = n // 2
    tables = []
    for m in range(1, n):
        tables.append(repaired(n, {i: i ^ m for i in range(n) if abs(i - (i ^ m)) <= reach}))
    up = repaired(n, {i: i ^ 2 for i in range(n)})
    middle = {}
    for pair in range(1, n // 2 - 1, 2):
        for c in range(2):
            middle[2 * pair + c], middle[2 * pair + 2 + c] = 2 * pair + 2 + c, 2 * pair + c
    return tables, up, repaired(n, middle)


def swap(x, table):
    return lax.ppermute(x, "ctx", list(enumerate(table)))


def local(
    kda_query,
    kda_key,
    kda_value,
    log_decay,
    write_rate,
    mla_query,
    latents,
    key_up,
    value_up,
    doc_lengths,
):
    rows = latents.shape[0]
    heads = write_rate.shape[1]
    n = lax.axis_size("ctx")
    ndocs = doc_lengths.shape[0]
    place = lax.axis_index("ctx")
    first_row = place * rows
    starts = (jnp.cumsum(doc_lengths) - doc_lengths).astype(jnp.int32)
    tables, up, middle = routes(n)
    partner = [i ^ 1 for i in range(n)]
    reach = n // 2
    window = reach + 1
    column = place % 2
    pair = place // 2
    half_groups = heads // 2 // GROUP

    def kda_half(which):
        scalars = jnp.concatenate(
            [jnp.stack([which * half_groups, first_row]).astype(jnp.int32), starts]
        )
        return kda_local(
            scalars, kda_query, kda_key, kda_value, log_decay, write_rate, half_groups, ndocs
        )

    mu_away, qe_away, lo_away = kda_half(1 - column)
    mu_got = swap(mu_away, partner)
    moved = [swap(latents, t) for t in tables]
    mu_own, qe_own, lo_own = kda_half(column)

    slots = np.full((n, n), -1, np.int32)
    for i in range(n):
        slots[i, 0] = window - 1
        for m, t in enumerate(tables):
            if 0 < i - t[i] <= reach:
                slots[i, m + 1] = window - 1 - (i - t[i])
    mla_scalars = jnp.concatenate(
        [first_row[None].astype(jnp.int32), jnp.asarray(slots)[place], starts]
    )

    def attend(first, groups, previous):
        return mla(
            mla_scalars,
            mla_query,
            key_up,
            value_up,
            [latents, *moved],
            window,
            ndocs,
            first,
            groups,
            previous,
        )

    where = jnp.stack([column, (pair == 0).astype(jnp.int32), pair % 2]).astype(jnp.int32)
    shape = (heads // 2, 128, 128)
    pm, pu = whole_call(pair_kernel, "pair_join", where, [mu_own, mu_got], [shape, shape])
    state = pu
    rounds = -(-n // 4)
    for step in range(rounds):
        a, b = swap(state, up), swap(state, middle)
        if step < rounds - 1:
            (state,) = whole_call(step_kernel, "pair_step", where, [pm, pu, a, b], [shape])
    s_own, s_send = whole_call(
        split_kernel, "slab_states", where, [mu_own, mu_got, a, b], [shape, shape]
    )
    s_got = swap(s_send, partner)
    all_groups = heads // GROUP
    mla_out = attend(0, all_groups // 2, None)
    mla_out = attend(all_groups // 2, all_groups // 2, mla_out)
    out = final(column[None].astype(jnp.int32), qe_own, lo_own, s_own, heads, None)
    kda_out = final((1 - column)[None].astype(jnp.int32), qe_away, lo_away, s_got, heads, out)
    return (kda_out, mla_out)


def solution(mesh):
    in_specs = (
        P(("batch", "ctx"), None),
        P(("batch", "ctx"), None),
        P(("batch", "ctx"), None),
        P(("batch", "ctx"), None),
        P(("batch", "ctx"), None),
        P(("batch", "ctx"), None),
        P(("batch", "ctx"), None),
        P(),
        P(),
        P("batch"),
    )
    out_specs = (P(("batch", "ctx"), None), P(("batch", "ctx"), None))
    return jax.shard_map(local, mesh=mesh, in_specs=in_specs, out_specs=out_specs, check_vma=False)
```

```python
import functools
import math

import jax
import jax.numpy as jnp
import numpy as np
from jax import lax
from jax.experimental import pallas as pl
from jax.experimental.pallas import tpu as pltpu
from jax.sharding import PartitionSpec as P

NOPE = 128
ROPE = 64
LATENT = 512
VMEM = 20 * 1024 * 1024
WHOLE = pl.BlockSpec(memory_space=pltpu.VMEM)
SCALARS = pl.BlockSpec(memory_space=pltpu.SMEM)
FAR = pl.BlockSpec(memory_space=pltpu.HBM)
BF = jnp.bfloat16
F32 = jnp.float32
NEG = -1e30


def mm(a, b):
    return jnp.dot(a, b, preferred_element_type=F32)


def mm_nt(a, b):
    return lax.dot_general(a, b, (((1,), (1,)), ((), ())), preferred_element_type=F32)


def mm_tn(a, b):
    return lax.dot_general(a, b, (((0,), (0,)), ((), ())), preferred_element_type=F32)


def doc_of(places, lengths_ref, ndocs):
    total = jnp.full(jnp.shape(places), -1, jnp.int32)
    start = 0
    for j in range(ndocs):
        total = total + (start <= places).astype(jnp.int32)
        start = start + lengths_ref[j]
    return total


def kda_kernel(ndocs, flip, sc, *refs):
    sources, (b_ref, mu_ref, qe_ref, lo_ref), blocks, sems = refs[:4], refs[4:8], refs[8:12], refs[12]
    rows, width = blocks[0].shape
    place = lax.axis_index("ctx")
    side = (place + flip) % 2
    start = pl.multiple_of(side * width, width)
    parts = 2
    part = width // parts
    copies = [
        [
            pltpu.make_async_copy(
                source.at[:, pl.ds(start + i * part, part)],
                block.at[:, pl.ds(i * part, part)],
                sems.at[j, i],
            )
            for j, (source, block) in enumerate(zip(sources, blocks))
        ]
        for i in range(parts)
    ]
    for group in copies:
        for copy in group:
            copy.start()
    q_ref, k_ref, v_ref, g_ref = blocks
    half = rows // 2
    heads = width // 128
    base = side * heads
    first = place * rows
    ri = lax.broadcasted_iota(jnp.int32, (rows, rows), 0)
    ci = lax.broadcasted_iota(jnp.int32, (rows, rows), 1)
    doc_r = doc_of(first + ri, sc, ndocs)
    doc_c = doc_of(first + ci, sc, ndocs)
    prev = doc_of(first - 1, sc, ndocs)
    last = doc_of(first + rows - 1, sc, ndocs)
    same = doc_r == doc_c
    strict = same & (ri > ci)
    causal = same & (ri >= ci)
    follow = (doc_r == prev).astype(F32)
    tail = (doc_r == last).astype(F32)
    keep = (last == prev).astype(F32)
    eye = (ri == ci).astype(F32)
    tri = (ri >= ci).astype(BF)
    low = ci < half

    hs = range(heads)
    lhs, km, lhs_off, km_off, rhs, kt, qg, gl, gain = [], [], [], [], [], [], [], [], []
    for h in hs:
        cols = slice(h * 128, (h + 1) * 128)
        if h % (heads // parts) == 0:
            i = h // (heads // parts)
            for copy in copies[i]:
                copy.wait()
            cum_part = mm(tri, g_ref[:, i * part : (i + 1) * part])
        q = q_ref[:, cols].astype(F32)
        k = k_ref[:, cols].astype(F32)
        v = v_ref[:, cols].astype(F32)
        qn = q * lax.rsqrt(jnp.sum(q * q, axis=1, keepdims=True) + 1e-06)
        kn = k * lax.rsqrt(jnp.sum(k * k, axis=1, keepdims=True) + 1e-06)
        cum = cum_part[:, h * 128 - i * part : (h + 1) * 128 - i * part]
        b = jnp.sum(eye * b_ref[pl.ds(base + h, 1), :], axis=1, keepdims=True)
        quarter = half // 2
        m0 = cum[quarter - 1 : quarter]
        m1 = cum[half + quarter - 1 : half + quarter]
        mid = cum[half - 1 : half]
        end = cum[rows - 1 : rows]
        c0, c1 = cum[:half], cum[half:]
        dp = jnp.concatenate([jnp.exp(c0 - m0), jnp.exp(c1 - m1)], axis=0)
        dm = jnp.concatenate([jnp.exp(m0 - c0), jnp.exp(m1 - c1)], axis=0)
        op = jnp.exp(c1 - mid)
        om = jnp.exp(jnp.minimum(mid - cum, 0.0))
        growth = jnp.exp(cum)
        trail = jnp.exp(end - cum)
        lhs.append(jnp.concatenate([(kn * dp).astype(BF), (qn * dp).astype(BF)], axis=0))
        km.append((kn * dm).astype(BF))
        lhs_off.append(
            jnp.concatenate([(kn[half:] * op).astype(BF), (qn[half:] * op).astype(BF)], axis=0)
        )
        km_off.append((kn * om).astype(BF))
        rhs.append(
            jnp.concatenate([(kn * growth * (b * follow)).astype(BF), (v * b).astype(BF)], axis=1)
        )
        kt.append((kn * trail * tail).astype(BF))
        qg.append(qn * growth * follow)
        gl.append(jnp.exp(end) * keep)
        gain.append(b)

    a, mix = [], []
    for h in hs:
        p = mm_nt(lhs[h], km[h])
        o = mm_nt(lhs_off[h], km_off[h])
        pa, pq = p[:rows], p[rows:]
        pa = jnp.concatenate([pa[:half], jnp.where(low[half:], o[:half], pa[half:])], axis=0)
        pq = jnp.concatenate([pq[:half], jnp.where(low[half:], o[half:], pq[half:])], axis=0)
        a.append(jnp.where(strict, pa, 0.0) * gain[h])
        mix.append(jnp.where(causal, pq, 0.0).astype(BF))

    t = [eye - jnp.where((ri >> 1) == (ci >> 1), a[h], 0.0) for h in hs]
    shift = 1
    while (2 << shift) <= rows:
        level = ((ri >> (shift + 1)) == (ci >> (shift + 1))) & ((ri >> shift) != (ci >> shift))
        tb = [t[h].astype(BF) for h in hs]
        x = [mm(jnp.where(level, a[h], 0.0).astype(BF), tb[h]).astype(BF) for h in hs]
        t = [t[h] - mm(tb[h], x[h]) for h in hs]
        shift += 1

    wu = [mm(t[h].astype(BF), rhs[h]).astype(BF) for h in hs]
    for h in hs:
        cols = slice(h * 128, (h + 1) * 128)
        z = mm_tn(kt[h], wu[h])
        mu_ref[h, :, :128] = (eye * gl[h] - z[:, :128]).astype(BF)
        mu_ref[h, :, 128:] = z[:, 128:].astype(BF)
        y = mm(mix[h], wu[h])
        qe_ref[:, cols] = (qg[h] - y[:, :128]).astype(BF)
        lo_ref[:, cols] = y[:, 128:]


def kda_half(flip, lengths, q, k, v, g, b):
    rows, width = q.shape[0], q.shape[1] // 2
    heads, ndocs = b.shape[0], lengths.shape[0]
    return pl.pallas_call(
        functools.partial(kda_kernel, ndocs, flip),
        in_specs=[SCALARS, FAR, FAR, FAR, FAR, WHOLE],
        out_specs=[WHOLE, WHOLE, WHOLE],
        out_shape=[
            jax.ShapeDtypeStruct((heads // 2, 128, 256), BF),
            jax.ShapeDtypeStruct((rows, width), BF),
            jax.ShapeDtypeStruct((rows, width), F32),
        ],
        scratch_shapes=[pltpu.VMEM((rows, width), BF)] * 4 + [pltpu.SemaphoreType.DMA((4, 2))],
        compiler_params=pltpu.CompilerParams(vmem_limit_bytes=VMEM),
        cost_estimate=pl.CostEstimate(
            flops=heads * 2 * 128**3 * 100, bytes_accessed=width * rows * 16, transcendentals=0
        ),
        name="kda_slab",
    )(lengths, q, k, v, g, b)


def pair_kernel(own_ref, got_ref, pm_ref, pu_ref):
    place = lax.axis_index("ctx")

    def go(first_ref, second_ref):
        for h in range(own_ref.shape[0]):
            z = mm(second_ref[h, :, :128], first_ref[h])
            pm_ref[h] = z[:, :128].astype(BF)
            pu_ref[h] = (z[:, 128:] + second_ref[h, :, 128:].astype(F32)).astype(BF)

    @pl.when(place % 2 == 0)
    def _():
        go(own_ref, got_ref)

    @pl.when(place % 2 == 1)
    def _():
        go(got_ref, own_ref)


def arrived(place, a_ref, b_ref, h):
    x = jnp.where((place // 2) % 2 == 1, a_ref[h].astype(F32), b_ref[h].astype(F32))
    return jnp.where(place < 2, 0.0, x).astype(BF)


def step_kernel(pm_ref, pu_ref, a_ref, b_ref, out_ref):
    place = lax.axis_index("ctx")
    for h in range(pm_ref.shape[0]):
        x = arrived(place, a_ref, b_ref, h)
        out_ref[h] = (mm(pm_ref[h], x) + pu_ref[h].astype(F32)).astype(BF)


def split_kernel(own_ref, got_ref, a_ref, b_ref, mine_ref, send_ref):
    place = lax.axis_index("ctx")

    def go(mu_ref, plain_ref, moved_ref):
        for h in range(own_ref.shape[0]):
            x = arrived(place, a_ref, b_ref, h)
            plain_ref[h] = x
            moved_ref[h] = (mm(mu_ref[h, :, :128], x) + mu_ref[h, :, 128:].astype(F32)).astype(BF)

    @pl.when(place % 2 == 0)
    def _():
        go(own_ref, mine_ref, send_ref)

    @pl.when(place % 2 == 1)
    def _():
        go(got_ref, send_ref, mine_ref)


def whole_call(kernel, name, args, outs):
    return pl.pallas_call(
        kernel,
        in_specs=[WHOLE] * len(args),
        out_specs=[WHOLE] * len(outs),
        out_shape=[jax.ShapeDtypeStruct(o, BF) for o in outs],
        compiler_params=pltpu.CompilerParams(vmem_limit_bytes=VMEM // 2),
        name=name,
    )(*args)


def final_kernel(flip, qe_ref, lo_ref, s_ref, *rest):
    out_ref, held_ref, sem = rest[-3:]
    width = qe_ref.shape[1]
    side = (lax.axis_index("ctx") + flip) % 2
    start = pl.multiple_of(side * width, width)
    parts = 2
    part = width // parts
    copies = []
    for h in range(s_ref.shape[0]):
        cols = slice(h * 128, (h + 1) * 128)
        held_ref[:, cols] = (lo_ref[:, cols] + mm(qe_ref[:, cols], s_ref[h])).astype(BF)
        if (h + 1) * 128 % part == 0:
            i = len(copies)
            copies.append(
                pltpu.make_async_copy(
                    held_ref.at[:, pl.ds(i * part, part)],
                    out_ref.at[:, pl.ds(start + i * part, part)],
                    sem.at[i],
                )
            )
            copies[-1].start()
    for copy in copies:
        copy.wait()


def final(flip, qe, lo, s, heads, previous):
    rows, width = qe.shape
    args, specs, aliases = [qe, lo, s], [WHOLE] * 3, {}
    if previous is not None:
        args.append(previous)
        specs.append(FAR)
        aliases = {3: 0}
    return pl.pallas_call(
        functools.partial(final_kernel, flip),
        in_specs=specs,
        out_specs=FAR,
        out_shape=jax.ShapeDtypeStruct((rows, heads * 128), BF),
        scratch_shapes=[pltpu.VMEM((rows, width), BF), pltpu.SemaphoreType.DMA((2,))],
        input_output_aliases=aliases,
        compiler_params=pltpu.CompilerParams(vmem_limit_bytes=VMEM // 2),
        name="kda_out",
    )(*args)


def window_rows(place, reach, rows, own_ref, mate_ref, far, out_ref):
    def put(w, block):
        at = slice(w * rows, (w + 1) * rows)
        out_ref[at, :LATENT] = block[:LATENT].T
        out_ref[at, LATENT:] = block[LATENT:].T

    for column in range(2):
        for parity in range(2):

            @pl.when((place % 2 == column) & ((place // 2) % 2 == parity))
            def _():
                for w in range(reach + 1):
                    back = reach // 2 - (w + column) // 2
                    other = ((w + column) % 2) ^ column
                    if back == 0:
                        put(w, (mate_ref if other else own_ref)[...])
                    else:
                        put(w, far[2 * (back - 1) + 1 - parity][other])


def mla_kernel(ndocs, reach, count, first, lengths, q_ref, ku_ref, vu_ref, *refs):
    out_ref, held_ref, bias_ref, sem = refs[-4:]
    place = lax.axis_index("ctx")
    rows = q_ref.shape[0]
    keys = (reach + 1) * rows
    if count is None:
        lat_ref = refs[0]
    else:
        own_ref, mate_ref, lat_ref = refs[0], refs[1], refs[2 + count]
        window_rows(place, reach, rows, own_ref, mate_ref, refs[2 : 2 + count], lat_ref)
    here = place * rows + lax.broadcasted_iota(jnp.int32, (rows, 1), 0)
    there = (place - reach) * rows + lax.broadcasted_iota(jnp.int32, (1, keys), 1)
    doc_q = doc_of(here, lengths, ndocs)
    doc_k = doc_of(there, lengths, ndocs)
    bias_ref[...] = jnp.where((there <= here) & (doc_q == doc_k), 0.0, NEG)

    factor = math.log2(math.e) / math.sqrt(NOPE + ROPE)
    lat = lat_ref[:, :LATENT]
    rope = lat_ref[:, LATENT:]
    width = held_ref.shape[1]
    part = slice(first * 128, first * 128 + width)
    kn = mm(lat, ku_ref[:, part]).astype(BF)
    vals = mm(lat, vu_ref[:, part]).astype(BF)
    bias = bias_ref[...]
    hs = range(width // 128)
    cols = [slice(h * 128, (h + 1) * 128) for h in hs]
    wide = NOPE + ROPE
    s = [
        mm_nt(
            q_ref[:, (first + h) * wide : (first + h + 1) * wide],
            jnp.concatenate([kn[:, cols[h]], rope], axis=1),
        )
        for h in hs
    ]
    s = [x * factor + bias for x in s]
    w = [jnp.exp2(x - jnp.max(x, axis=1, keepdims=True)) for x in s]
    for h in hs:
        total = jnp.sum(w[h], axis=1, keepdims=True)
        held_ref[:, cols[h]] = (mm(w[h].astype(BF), vals[:, cols[h]]) / total).astype(BF)
    copy = pltpu.make_async_copy(held_ref, out_ref.at[:, part], sem)
    copy.start()
    copy.wait()


def mla(lengths, q, ku, vu, blocks, previous, reach, first, count):
    rows = q.shape[0]
    heads = ku.shape[1] // NOPE
    keys = (reach + 1) * rows
    args = [lengths, q, ku, vu, *blocks]
    specs = [SCALARS] + [WHOLE] * (len(args) - 1)
    out = jax.ShapeDtypeStruct((rows, heads * 128), BF)
    aliases = {}
    if previous is not None:
        aliases = {len(args): 0}
        args.append(previous)
        specs.append(FAR)
    return pl.pallas_call(
        functools.partial(
            mla_kernel,
            lengths.shape[0],
            reach,
            len(blocks) - 2 if previous is None else None,
            first,
        ),
        in_specs=specs,
        out_specs=[WHOLE, FAR] if previous is None else FAR,
        out_shape=[jax.ShapeDtypeStruct((keys, LATENT + ROPE), BF), out]
        if previous is None
        else out,
        scratch_shapes=[
            pltpu.VMEM((rows, count * 128), BF),
            pltpu.VMEM((rows, keys), F32),
            pltpu.SemaphoreType.DMA,
        ],
        input_output_aliases=aliases,
        compiler_params=pltpu.CompilerParams(vmem_limit_bytes=VMEM),
        cost_estimate=pl.CostEstimate(
            flops=6 * keys * count * 128 * (2 * LATENT + 3 * rows),
            bytes_accessed=count * 128 * 3000,
            transcendentals=0,
        ),
        name="mla_heads",
    )(*args)


def repaired(n, wanted):
    left = [i for i in range(n) if i not in wanted]
    out = dict(wanted)
    for a, b in zip(left[::2], left[1::2]):
        out[a], out[b] = b, a
    return [out[i] for i in range(n)]


def routes(n):
    mate = [i ^ 1 for i in range(n)]
    up = repaired(n, {i: i ^ 2 for i in range(n)})
    middle = {}
    for pair in range(1, n // 2 - 1, 2):
        for c in range(2):
            middle[2 * pair + c], middle[2 * pair + 2 + c] = 2 * pair + 2 + c, 2 * pair + c
    return mate, up, repaired(n, middle)


def swap(x, table):
    return lax.ppermute(x, "ctx", list(enumerate(table)))


def local(
    kda_query,
    kda_key,
    kda_value,
    log_decay,
    write_rate,
    mla_query,
    latents,
    key_up,
    value_up,
    doc_lengths,
):
    n = lax.axis_size("ctx")
    heads = write_rate.shape[1]
    reach = n // 2
    rounds = -(-n // 4)
    mate, up, middle = routes(n)
    kda_args = (doc_lengths, kda_query, kda_key, kda_value, log_decay, write_rate.T)

    lat = latents.T
    lat_mate = swap(lat, mate)
    mu_away, qe_away, lo_away = kda_half(1, *kda_args)
    mu_got = swap(mu_away, mate)
    lat_mate, _ = lax.optimization_barrier((lat_mate, mu_away))
    both = jnp.stack([lat, lat_mate])
    blocks = [lat, lat_mate]
    a = b = both
    for _ in range(rounds):
        a, b = swap(b, up), swap(a, middle)
        blocks += [a, b]
    mu_own, qe_own, lo_own = kda_half(0, *kda_args)

    def attend(latent_blocks, previous, first, count):
        return mla(
            doc_lengths,
            mla_query,
            key_up,
            value_up,
            latent_blocks,
            previous,
            reach,
            first,
            count,
        )

    shape = (heads // 2, 128, 128)
    pm, pu = whole_call(pair_kernel, "pair_join", [mu_own, mu_got], [shape, shape])
    state = pu
    for step in range(rounds):
        a, b = swap(state, up), swap(state, middle)
        if step == 0:
            window, mla_out = attend(blocks, None, 0, heads // 2)
            a, b, window = lax.optimization_barrier((a, b, window))
        if step < rounds - 1:
            (state,) = whole_call(step_kernel, "pair_step", [pm, pu, a, b], [shape])
    mla_out = attend([window], mla_out, heads // 2, heads // 2)
    a, b, mla_out = lax.optimization_barrier((a, b, mla_out))
    s_own, s_send = whole_call(split_kernel, "slab_states", [mu_own, mu_got, a, b], [shape, shape])
    s_got = swap(s_send, mate)
    out = final(0, qe_own, lo_own, s_own, heads, None)
    kda_out = final(1, qe_away, lo_away, s_got, heads, out)
    return (kda_out, mla_out)


def solution(mesh):
    in_specs = (
        P(("batch", "ctx"), None),
        P(("batch", "ctx"), None),
        P(("batch", "ctx"), None),
        P(("batch", "ctx"), None),
        P(("batch", "ctx"), None),
        P(("batch", "ctx"), None),
        P(("batch", "ctx"), None),
        P(),
        P(),
        P("batch"),
    )
    out_specs = (P(("batch", "ctx"), None), P(("batch", "ctx"), None))
    return jax.shard_map(local, mesh=mesh, in_specs=in_specs, out_specs=out_specs, check_vma=False)
```

```python
import functools
import math

import jax
import jax.numpy as jnp
import numpy as np
from jax import lax
from jax.experimental import pallas as pl
from jax.experimental.pallas import tpu as pltpu
from jax.sharding import PartitionSpec as P

NOPE = 128
ROPE = 64
LATENT = 512
VMEM = 20 * 1024 * 1024
ALL_VMEM = 56 * 1024 * 1024
WHOLE = pl.BlockSpec(memory_space=pltpu.VMEM)
SCALARS = pl.BlockSpec(memory_space=pltpu.SMEM)
FAR = pl.BlockSpec(memory_space=pltpu.HBM)
BF = jnp.bfloat16
F32 = jnp.float32
NEG = -1e30


def mm(a, b):
    return jnp.dot(a, b, preferred_element_type=F32)


def mm_nt(a, b):
    return lax.dot_general(a, b, (((1,), (1,)), ((), ())), preferred_element_type=F32)


def mm_tn(a, b):
    return lax.dot_general(a, b, (((0,), (0,)), ((), ())), preferred_element_type=F32)


def doc_of(places, lengths_ref, ndocs):
    total = jnp.full(jnp.shape(places), -1, jnp.int32)
    start = 0
    for j in range(ndocs):
        total = total + (start <= places).astype(jnp.int32)
        start = start + lengths_ref[j]
    return total


def kda_kernel(ndocs, flip, *refs):
    sources, small = refs[:4], refs[4:6]
    mu_ref, qe_ref, lo_ref = refs[6:9]
    blocks, (b_ref, sc, sems, small_sems) = refs[9:13], refs[13:]
    rows, width = blocks[0].shape
    place = lax.axis_index("ctx")
    side = (place + flip) % 2
    start = pl.multiple_of(side * width, width)
    parts = sems.shape[1]
    part = width // parts
    small_copies = [
        pltpu.make_async_copy(source, block, small_sems.at[j])
        for j, (source, block) in enumerate(zip(small, (sc, b_ref)))
    ]
    copies = [
        [
            pltpu.make_async_copy(
                source.at[:, pl.ds(start + i * part, part)],
                block.at[:, pl.ds(i * part, part)],
                sems.at[j, i],
            )
            for j, (source, block) in enumerate(zip(sources, blocks))
        ]
        for i in range(parts)
    ]
    for copy in small_copies:
        copy.start()
    for group in copies:
        for copy in group:
            copy.start()
    q_ref, k_ref, v_ref, g_ref = blocks
    half = rows // 2
    heads = width // 128
    base = side * heads
    first = place * rows
    ri = lax.broadcasted_iota(jnp.int32, (rows, rows), 0)
    ci = lax.broadcasted_iota(jnp.int32, (rows, rows), 1)
    tri = (ri >= ci).astype(BF)
    low = ci < half
    eye = (ri == ci).astype(F32)

    hs = range(heads)
    kept, lhs, km, lhs_off, km_off = [], [], [], [], []
    for h in hs:
        cols = slice(h * 128, (h + 1) * 128)
        if h % (heads // parts) == 0:
            i = h // (heads // parts)
            for copy in copies[i]:
                copy.wait()
            cum_part = mm(tri, g_ref[:, i * part : (i + 1) * part])
        q = q_ref[:, cols].astype(F32)
        k = k_ref[:, cols].astype(F32)
        qn = q * lax.rsqrt(jnp.sum(q * q, axis=1, keepdims=True) + 1e-06)
        kn = k * lax.rsqrt(jnp.sum(k * k, axis=1, keepdims=True) + 1e-06)
        cum = cum_part[:, h * 128 - i * part : (h + 1) * 128 - i * part]
        quarter = half // 2
        m0 = cum[quarter - 1 : quarter]
        m1 = cum[half + quarter - 1 : half + quarter]
        mid = cum[half - 1 : half]
        end = cum[rows - 1 : rows]
        c0, c1 = cum[:half], cum[half:]
        dp = jnp.concatenate([jnp.exp(c0 - m0), jnp.exp(c1 - m1)], axis=0)
        dm = jnp.concatenate([jnp.exp(m0 - c0), jnp.exp(m1 - c1)], axis=0)
        op = jnp.exp(c1 - mid)
        om = jnp.exp(jnp.minimum(mid - cum, 0.0))
        growth = jnp.exp(cum)
        trail = jnp.exp(end - cum)
        lhs.append(jnp.concatenate([(kn * dp).astype(BF), (qn * dp).astype(BF)], axis=0))
        km.append((kn * dm).astype(BF))
        lhs_off.append(
            jnp.concatenate([(kn[half:] * op).astype(BF), (qn[half:] * op).astype(BF)], axis=0)
        )
        km_off.append((kn * om).astype(BF))
        kept.append((kn * growth, kn * trail, qn * growth, jnp.exp(end)))

    for copy in small_copies:
        copy.wait()
    doc_r = doc_of(first + ri, sc, ndocs)
    doc_c = doc_of(first + ci, sc, ndocs)
    prev = doc_of(first - 1, sc, ndocs)
    last = doc_of(first + rows - 1, sc, ndocs)
    same = doc_r == doc_c
    strict = same & (ri > ci)
    causal = same & (ri >= ci)
    follow = (doc_r == prev).astype(F32)
    tail = (doc_r == last).astype(F32)
    keep = (last == prev).astype(F32)
    rhs, kt, qg, gl, gain = [], [], [], [], []
    for h in hs:
        grown, trailed, queried, ended = kept[h]
        b = jnp.sum(eye * b_ref[pl.ds(base + h, 1), :], axis=1, keepdims=True)
        v = v_ref[:, h * 128 : (h + 1) * 128].astype(F32)
        rhs.append(
            jnp.concatenate([(grown * (b * follow)).astype(BF), (v * b).astype(BF)], axis=1)
        )
        kt.append((trailed * tail).astype(BF))
        qg.append(queried * follow)
        gl.append(ended * keep)
        gain.append(b)

    a, mix = [], []
    for h in hs:
        p = mm_nt(lhs[h], km[h])
        o = mm_nt(lhs_off[h], km_off[h])
        pa, pq = p[:rows], p[rows:]
        pa = jnp.concatenate([pa[:half], jnp.where(low[half:], o[:half], pa[half:])], axis=0)
        pq = jnp.concatenate([pq[:half], jnp.where(low[half:], o[half:], pq[half:])], axis=0)
        a.append(jnp.where(strict, pa, 0.0) * gain[h])
        mix.append(jnp.where(causal, pq, 0.0).astype(BF))

    t = [eye - jnp.where((ri >> 1) == (ci >> 1), a[h], 0.0) for h in hs]
    shift = 1
    while (2 << shift) <= rows:
        level = ((ri >> (shift + 1)) == (ci >> (shift + 1))) & ((ri >> shift) != (ci >> shift))
        tb = [t[h].astype(BF) for h in hs]
        x = [mm(jnp.where(level, a[h], 0.0).astype(BF), tb[h]).astype(BF) for h in hs]
        t = [t[h] - mm(tb[h], x[h]) for h in hs]
        shift += 1

    wu = [mm(t[h].astype(BF), rhs[h]).astype(BF) for h in hs]
    for h in hs:
        cols = slice(h * 128, (h + 1) * 128)
        z = mm_tn(kt[h], wu[h])
        mu_ref[h, :, :128] = (eye * gl[h] - z[:, :128]).astype(BF)
        mu_ref[h, :, 128:] = z[:, 128:].astype(BF)
        y = mm(mix[h], wu[h])
        qe_ref[:, cols] = (qg[h] - y[:, :128]).astype(BF)
        lo_ref[:, cols] = y[:, 128:]


def kda_half(flip, lengths, q, k, v, g, b):
    rows, width = q.shape[0], q.shape[1] // 2
    heads, ndocs = b.shape[0], lengths.shape[0]
    return pl.pallas_call(
        functools.partial(kda_kernel, ndocs, flip),
        in_specs=[FAR] * 6,
        out_specs=[WHOLE, WHOLE, WHOLE],
        out_shape=[
            jax.ShapeDtypeStruct((heads // 2, 128, 256), BF),
            jax.ShapeDtypeStruct((rows, width), BF),
            jax.ShapeDtypeStruct((rows, width), F32),
        ],
        scratch_shapes=[pltpu.VMEM((rows, width), BF)] * 4
        + [
            pltpu.VMEM(b.shape, F32),
            pltpu.SMEM(lengths.shape, jnp.int32),
            pltpu.SemaphoreType.DMA((4, 4)),
            pltpu.SemaphoreType.DMA((2,)),
        ],
        compiler_params=pltpu.CompilerParams(vmem_limit_bytes=ALL_VMEM if flip else VMEM),
        cost_estimate=pl.CostEstimate(
            flops=heads * 2 * 128**3 * 100, bytes_accessed=width * rows * 16, transcendentals=0
        ),
        name="kda_slab",
    )(q, k, v, g, lengths, b)


def pair_kernel(own_ref, got_ref, pm_ref, pu_ref):
    place = lax.axis_index("ctx")

    def go(first_ref, second_ref):
        for h in range(own_ref.shape[0]):
            z = mm(second_ref[h, :, :128], first_ref[h])
            pm_ref[h] = z[:, :128].astype(BF)
            pu_ref[h] = (z[:, 128:] + second_ref[h, :, 128:].astype(F32)).astype(BF)

    @pl.when(place % 2 == 0)
    def _():
        go(own_ref, got_ref)

    @pl.when(place % 2 == 1)
    def _():
        go(got_ref, own_ref)


def arrived(place, a_ref, b_ref, h):
    x = jnp.where((place // 2) % 2 == 1, a_ref[h].astype(F32), b_ref[h].astype(F32))
    return jnp.where(place < 2, 0.0, x).astype(BF)


def step_kernel(pm_ref, pu_ref, a_ref, b_ref, out_ref):
    place = lax.axis_index("ctx")
    for h in range(pm_ref.shape[0]):
        x = arrived(place, a_ref, b_ref, h)
        out_ref[h] = (mm(pm_ref[h], x) + pu_ref[h].astype(F32)).astype(BF)


def split_kernel(own_ref, got_ref, a_ref, b_ref, mine_ref, send_ref):
    place = lax.axis_index("ctx")

    def go(mu_ref, plain_ref, moved_ref):
        for h in range(own_ref.shape[0]):
            x = arrived(place, a_ref, b_ref, h)
            plain_ref[h] = x
            moved_ref[h] = (mm(mu_ref[h, :, :128], x) + mu_ref[h, :, 128:].astype(F32)).astype(BF)

    @pl.when(place % 2 == 0)
    def _():
        go(own_ref, mine_ref, send_ref)

    @pl.when(place % 2 == 1)
    def _():
        go(got_ref, send_ref, mine_ref)


def whole_call(kernel, name, args, outs):
    return pl.pallas_call(
        kernel,
        in_specs=[WHOLE] * len(args),
        out_specs=[WHOLE] * len(outs),
        out_shape=[jax.ShapeDtypeStruct(o, BF) for o in outs],
        compiler_params=pltpu.CompilerParams(vmem_limit_bytes=VMEM // 2),
        name=name,
    )(*args)


def final_kernel(flip, qe_ref, lo_ref, s_ref, *rest):
    out_ref, held_ref, sem = rest[-3:]
    width = qe_ref.shape[1]
    side = (lax.axis_index("ctx") + flip) % 2
    start = pl.multiple_of(side * width, width)
    parts = 2
    part = width // parts
    copies = []
    for h in range(s_ref.shape[0]):
        cols = slice(h * 128, (h + 1) * 128)
        held_ref[:, cols] = (lo_ref[:, cols] + mm(qe_ref[:, cols], s_ref[h])).astype(BF)
        if (h + 1) * 128 % part == 0:
            i = len(copies)
            copies.append(
                pltpu.make_async_copy(
                    held_ref.at[:, pl.ds(i * part, part)],
                    out_ref.at[:, pl.ds(start + i * part, part)],
                    sem.at[i],
                )
            )
            copies[-1].start()
    for copy in copies:
        copy.wait()


def final(flip, qe, lo, s, heads, previous):
    rows, width = qe.shape
    args, specs, aliases = [qe, lo, s], [WHOLE] * 3, {}
    if previous is not None:
        args.append(previous)
        specs.append(FAR)
        aliases = {3: 0}
    return pl.pallas_call(
        functools.partial(final_kernel, flip),
        in_specs=specs,
        out_specs=FAR,
        out_shape=jax.ShapeDtypeStruct((rows, heads * 128), BF),
        scratch_shapes=[pltpu.VMEM((rows, width), BF), pltpu.SemaphoreType.DMA((2,))],
        input_output_aliases=aliases,
        compiler_params=pltpu.CompilerParams(vmem_limit_bytes=VMEM // 2),
        name="kda_out",
    )(*args)


def window_rows(place, reach, rows, own_ref, mate_ref, out_ref):
    for column in range(2):

        @pl.when(place % 2 == column)
        def _():
            for w in range(reach + 1):
                back = reach // 2 - (w + column) // 2
                block = (mate_ref if (w + column) % 2 != column else own_ref)[back]
                at = slice(w * rows, (w + 1) * rows)
                out_ref[at, :LATENT] = block[:LATENT].T
                out_ref[at, LATENT:] = block[LATENT:].T


def pick_kernel(own_ref, *refs):
    out_ref = refs[-1]
    out_ref[0] = own_ref[...]
    parity = (lax.axis_index("ctx") // 2) % 2
    for back in range(out_ref.shape[0] - 1):
        for kind in range(2):

            @pl.when(parity == 1 - kind)
            def _():
                out_ref[back + 1] = refs[2 * back + kind][...]


def mask_kernel(ndocs, lengths, bias_ref):
    rows, keys = bias_ref.shape
    place = lax.axis_index("ctx")
    here = place * rows + lax.broadcasted_iota(jnp.int32, (rows, 1), 0)
    there = (place + 1) * rows - keys + lax.broadcasted_iota(jnp.int32, (1, keys), 1)
    doc_q = doc_of(here, lengths, ndocs)
    doc_k = doc_of(there, lengths, ndocs)
    bias_ref[...] = jnp.where((there <= here) & (doc_q == doc_k), 0.0, NEG)


def mask(lengths, rows, keys):
    return pl.pallas_call(
        functools.partial(mask_kernel, lengths.shape[0]),
        in_specs=[SCALARS],
        out_specs=WHOLE,
        out_shape=jax.ShapeDtypeStruct((rows, keys), F32),
        compiler_params=pltpu.CompilerParams(vmem_limit_bytes=VMEM // 2),
        name="window_mask",
    )(lengths)


def mla_kernel(reach, fresh, first, bias_ref, q_ref, ku_ref, vu_ref, *refs):
    out_ref, held_ref, sem = refs[-3:]
    rows = q_ref.shape[0]
    if not fresh:
        lat_ref = refs[0]
    else:
        lat_ref = refs[2]
        window_rows(lax.axis_index("ctx"), reach, rows, *refs[:2], lat_ref)

    factor = math.log2(math.e) / math.sqrt(NOPE + ROPE)
    lat = lat_ref[:, :LATENT]
    rope = lat_ref[:, LATENT:]
    width = held_ref.shape[1]
    part = slice(first * 128, first * 128 + width)
    kn = mm(lat, ku_ref[:, part]).astype(BF)
    vals = mm(lat, vu_ref[:, part]).astype(BF)
    bias = bias_ref[...]
    hs = range(width // 128)
    cols = [slice(h * 128, (h + 1) * 128) for h in hs]
    wide = NOPE + ROPE
    s = [
        mm_nt(
            q_ref[:, (first + h) * wide : (first + h + 1) * wide],
            jnp.concatenate([kn[:, cols[h]], rope], axis=1),
        )
        for h in hs
    ]
    s = [x * factor + bias for x in s]
    w = [jnp.exp2(x - jnp.max(x, axis=1, keepdims=True)) for x in s]
    for h in hs:
        total = jnp.sum(w[h], axis=1, keepdims=True)
        held_ref[:, cols[h]] = (mm(w[h].astype(BF), vals[:, cols[h]]) / total).astype(BF)
    copy = pltpu.make_async_copy(held_ref, out_ref.at[:, part], sem)
    copy.start()
    copy.wait()


def mla(bias, q, ku, vu, blocks, previous, reach, first, count):
    rows = q.shape[0]
    heads = ku.shape[1] // NOPE
    keys = (reach + 1) * rows
    args = [bias, q, ku, vu, *blocks]
    specs = [WHOLE] * len(args)
    out = jax.ShapeDtypeStruct((rows, heads * 128), BF)
    aliases = {}
    if previous is not None:
        aliases = {len(args): 0}
        args.append(previous)
        specs.append(FAR)
    return pl.pallas_call(
        functools.partial(
            mla_kernel,
            reach,
            previous is None,
            first,
        ),
        in_specs=specs,
        out_specs=[WHOLE, FAR] if previous is None else FAR,
        out_shape=[jax.ShapeDtypeStruct((keys, LATENT + ROPE), BF), out]
        if previous is None
        else out,
        scratch_shapes=[
            pltpu.VMEM((rows, count * 128), BF),
            pltpu.SemaphoreType.DMA,
        ],
        input_output_aliases=aliases,
        compiler_params=pltpu.CompilerParams(vmem_limit_bytes=VMEM),
        cost_estimate=pl.CostEstimate(
            flops=6 * keys * count * 128 * (2 * LATENT + 3 * rows),
            bytes_accessed=count * 128 * 3000,
            transcendentals=0,
        ),
        name="mla_heads",
    )(*args)


def routes(n):
    mate = [i ^ 1 for i in range(n)]
    up = [i ^ 2 for i in range(n)]
    middle = {}
    for pair in range(1, n // 2 - 1, 2):
        for c in range(2):
            middle[2 * pair + c], middle[2 * pair + 2 + c] = 2 * pair + 2 + c, 2 * pair + c
    return mate, up, middle


def swap(x, table):
    n, m = lax.axis_size("ctx"), lax.axis_size("batch")
    if isinstance(table, list):
        return lax.ppermute(x, "ctx", list(enumerate(table)))
    pairs = []
    for i in range(n):
        for j in range(m):
            pairs.append((i * m + j, table[i] * m + j if i in table else i * m + (j ^ 1)))
    return lax.ppermute(x, ("ctx", "batch"), pairs)


def local(
    kda_query,
    kda_key,
    kda_value,
    log_decay,
    write_rate,
    mla_query,
    latents,
    key_up,
    value_up,
    doc_lengths,
):
    n = lax.axis_size("ctx")
    heads = write_rate.shape[1]
    reach = n // 2
    rounds = -(-n // 4)
    mate, up, middle = routes(n)
    kda_args = (doc_lengths, kda_query, kda_key, kda_value, log_decay, write_rate.T)

    lat = latents.T
    shape = (heads // 2, 128, 128)
    mu_away, qe_away, lo_away = kda_half(1, *kda_args)
    mu_got = swap(mu_away, mate)
    mu_own, qe_own, lo_own = kda_half(0, *kda_args)
    early, _ = lax.optimization_barrier((lat, mu_away))
    moved = [(swap(early, up), swap(early, middle))]
    mu_own, *moved[0] = lax.optimization_barrier((mu_own, *moved[0]))
    for _ in range(rounds - 1):
        a, b = moved[-1]
        moved.append((swap(b, up), swap(a, middle)))
    (lat_own,) = whole_call(
        pick_kernel,
        "pick_latents",
        [lat, *[x for ab in moved for x in ab]],
        [(rounds + 1, *lat.shape)],
    )
    lat_mate = swap(lat_own, mate)
    pm, pu = whole_call(pair_kernel, "pair_join", [mu_own, mu_got], [shape, shape])
    later, _ = lax.optimization_barrier((doc_lengths, mu_own))
    bias = mask(later, latents.shape[0], (reach + 1) * latents.shape[0])

    def attend(latent_blocks, previous, first, count):
        return mla(
            bias,
            mla_query,
            key_up,
            value_up,
            latent_blocks,
            previous,
            reach,
            first,
            count,
        )

    state = pu
    for step in range(rounds):
        a, b = swap(state, up), swap(state, middle)
        if step < rounds - 1:
            (state,) = whole_call(step_kernel, "pair_step", [pm, pu, a, b], [shape])
    lat_own, _ = lax.optimization_barrier((lat_own, state))
    window, mla_out = attend([lat_own, lat_mate], None, 0, heads // 2)
    a, b, window = lax.optimization_barrier((a, b, window))
    s_own, s_send = whole_call(split_kernel, "slab_states", [mu_own, mu_got, a, b], [shape, shape])
    s_got = swap(s_send, mate)
    window, _ = lax.optimization_barrier((window, s_send))
    mla_out = attend([window], mla_out, heads // 2, heads // 2)
    out = final(0, qe_own, lo_own, s_own, heads, None)
    s_got, mla_out = lax.optimization_barrier((s_got, mla_out))
    kda_out = final(1, qe_away, lo_away, s_got, heads, out)
    return (kda_out, mla_out)


def solution(mesh):
    in_specs = (
        P(("batch", "ctx"), None),
        P(("batch", "ctx"), None),
        P(("batch", "ctx"), None),
        P(("batch", "ctx"), None),
        P(("batch", "ctx"), None),
        P(("batch", "ctx"), None),
        P(("batch", "ctx"), None),
        P(),
        P(),
        P("batch"),
    )
    out_specs = (P(("batch", "ctx"), None), P(("batch", "ctx"), None))
    return jax.shard_map(local, mesh=mesh, in_specs=in_specs, out_specs=out_specs, check_vma=False)
```

```python
import functools
import math

import jax
import jax.numpy as jnp
import numpy as np
from jax import lax
from jax.experimental import pallas as pl
from jax.experimental.pallas import tpu as pltpu
from jax.sharding import PartitionSpec as P

NOPE = 128
ROPE = 64
LATENT = 512
VMEM = 20 * 1024 * 1024
ALL_VMEM = 56 * 1024 * 1024
WHOLE = pl.BlockSpec(memory_space=pltpu.VMEM)
SCALARS = pl.BlockSpec(memory_space=pltpu.SMEM)
FAR = pl.BlockSpec(memory_space=pltpu.HBM)
CHEAP = pl.CostEstimate(flops=0, bytes_accessed=0, transcendentals=0)
BF = jnp.bfloat16
F32 = jnp.float32
NEG = -1e30


def mm(a, b):
    return jnp.dot(a, b, preferred_element_type=F32)


def mm_nt(a, b):
    return lax.dot_general(a, b, (((1,), (1,)), ((), ())), preferred_element_type=F32)


def mm_tn(a, b):
    return lax.dot_general(a, b, (((0,), (0,)), ((), ())), preferred_element_type=F32)


def doc_of(places, lengths_ref, ndocs):
    total = jnp.full(jnp.shape(places), -1, jnp.int32)
    start = 0
    for j in range(ndocs):
        total = total + (start <= places).astype(jnp.int32)
        start = start + lengths_ref[j]
    return total


def kda_kernel(ndocs, flip, states, outputs, *refs):
    names = [name for name in "gkqv" if name != "q" or outputs]
    sources, small = refs[: len(names)], refs[len(names) : len(names) + 2]
    refs = refs[len(names) + 2 :]
    if states:
        mu_ref, refs = refs[0], refs[1:]
    if outputs:
        qe_ref, lo_ref, refs = refs[0], refs[1], refs[2:]
    blocks, (b_ref, sc, sems, small_sems) = refs[: len(names)], refs[len(names) :]
    block = dict(zip(names, blocks))
    rows, width = blocks[0].shape
    place = lax.axis_index("ctx")
    side = (place + flip) % 2
    start = pl.multiple_of(side * width, width)
    copies = [
        pltpu.make_async_copy(source.at[:, pl.ds(start, width)], to, sems.at[j])
        for j, (source, to) in enumerate(zip(sources, blocks))
    ] + [
        pltpu.make_async_copy(source, to, small_sems.at[j])
        for j, (source, to) in enumerate(zip(small, (sc, b_ref)))
    ]
    for copy in copies:
        copy.start()
    half = rows // 2
    heads = width // 128
    base = side * heads
    first = place * rows
    ri = lax.broadcasted_iota(jnp.int32, (rows, rows), 0)
    ci = lax.broadcasted_iota(jnp.int32, (rows, rows), 1)
    tri = (ri >= ci).astype(BF)
    low = ci < half
    eye = (ri == ci).astype(F32)
    zeros = jnp.zeros((half, 128), BF)
    for copy in copies[: len(names) - 1]:
        copy.wait()
    cum_all = mm(tri, block["g"][...])

    def halves(top, bottom):
        return jnp.concatenate(
            [jnp.broadcast_to(top, (half, 128)), jnp.broadcast_to(bottom, (half, 128))], axis=0
        )

    hs = range(heads)
    kept, lhs, km, lhs_off, km_off = [], [], [], [], []
    for h in hs:
        cols = slice(h * 128, (h + 1) * 128)
        k = block["k"][:, cols].astype(F32)
        kn = k * lax.rsqrt(jnp.sum(k * k, axis=1, keepdims=True) + 1e-06)
        cum = cum_all[:, cols]
        quarter = half // 2
        m0 = cum[quarter - 1 : quarter]
        m1 = cum[half + quarter - 1 : half + quarter]
        mid = cum[half - 1 : half]
        end = cum[rows - 1 : rows]
        about = cum - halves(m0, m1)
        dp = jnp.exp(about)
        kd = kn * dp
        ku = kn * jnp.exp(-about)
        late = jnp.exp(m1 - mid)
        grow = halves(jnp.exp(m0 * 0.5), jnp.exp(m1 * 0.5))
        wane = halves(jnp.exp((end - m0) * 0.5), jnp.exp((end - m1) * 0.5))
        left, left_off = [kd.astype(BF)], [(kd[half:] * late).astype(BF)]
        queried = None
        if outputs:
            q = block["q"][:, cols].astype(F32)
            qd = q * lax.rsqrt(jnp.sum(q * q, axis=1, keepdims=True) + 1e-06) * dp
            left.append(qd.astype(BF))
            left_off.append((qd[half:] * late).astype(BF))
            queried = qd * grow * grow
        lhs.append(jnp.concatenate(left, axis=0))
        lhs_off.append(jnp.concatenate(left_off, axis=0))
        km.append(ku.astype(BF))
        km_off.append(
            jnp.concatenate([(ku[:half] * jnp.exp(mid - m0)).astype(BF), zeros], axis=0)
        )
        kept.append((kd * grow * grow, ku * wane * wane, queried, jnp.exp(end)))

    for copy in copies[len(names) - 1 :]:
        copy.wait()
    doc_r = doc_of(first + ri, sc, ndocs)
    doc_c = doc_of(first + ci, sc, ndocs)
    prev = doc_of(first - 1, sc, ndocs)
    last = doc_of(first + rows - 1, sc, ndocs)
    same = doc_r == doc_c
    strict = same & (ri > ci)
    causal = same & (ri >= ci)
    follow = (doc_r == prev).astype(F32)
    tail = (doc_r == last).astype(F32)
    keep = (last == prev).astype(F32)
    a, mix, rhs = [], [], []
    for h in hs:
        p = mm_nt(lhs[h], km[h])
        o = mm_nt(lhs_off[h], km_off[h])
        b = jnp.sum(eye * b_ref[pl.ds(base + h, 1), :], axis=1, keepdims=True)
        pa = jnp.concatenate([p[:half], jnp.where(low[half:], o[:half], p[half:rows])], axis=0)
        a.append(jnp.where(strict, pa * b, 0.0))
        if outputs:
            pq = p[rows:]
            pq = jnp.concatenate([pq[:half], jnp.where(low[half:], o[half:], pq[half:])], axis=0)
            mix.append(jnp.where(causal, pq, 0.0).astype(BF))
        v = block["v"][:, h * 128 : (h + 1) * 128].astype(F32)
        rhs.append(
            jnp.concatenate([(kept[h][0] * (b * follow)).astype(BF), (v * b).astype(BF)], axis=1)
        )

    t = [(eye - jnp.where((ri >> 1) == (ci >> 1), a[h], 0.0)).astype(BF) for h in hs]
    a = [a[h].astype(BF) for h in hs]
    bits, low_bit = rows.bit_length() - 1, 1
    while low_bit < bits:
        up_bit = min(low_bit + 3, bits)
        rest = ((ri >> up_bit) == (ci >> up_bit)) & ((ri >> low_bit) != (ci >> low_bit))
        rest = rest.astype(BF)
        w = [mm(a[h] * rest, t[h]).astype(BF) for h in hs]
        left = t
        for step in range(up_bit - low_bit):
            if step + 1 < up_bit - low_bit:
                z = [mm(jnp.concatenate([left[h], w[h]], axis=0), w[h]) for h in hs]
                w = [z[h][rows:].astype(BF) for h in hs]
                z = [z[h][:rows] for h in hs]
            else:
                z = [mm(left[h], w[h]) for h in hs]
            t = [t[h] - z[h] if step == 0 else t[h] + z[h] for h in hs]
            left = [t[h].astype(BF) for h in hs]
        t = left
        low_bit = up_bit

    wu = [mm(t[h], rhs[h]).astype(BF) for h in hs]
    for h in hs:
        cols = slice(h * 128, (h + 1) * 128)
        if states:
            z = mm_tn((kept[h][1] * tail).astype(BF), wu[h])
            mu_ref[h, :, :128] = (eye * (kept[h][3] * keep) - z[:, :128]).astype(BF)
            mu_ref[h, :, 128:] = z[:, 128:].astype(BF)
        if outputs:
            y = mm(mix[h], wu[h])
            qe_ref[:, cols] = (kept[h][2] * follow - y[:, :128]).astype(BF)
            lo_ref[:, cols] = y[:, 128:]


def kda_half(flip, lengths, q, k, v, g, b, states=True, outputs=True, limit=VMEM):
    rows, width = q.shape[0], q.shape[1] // 2
    heads, ndocs = b.shape[0], lengths.shape[0]
    args = [g, k] + ([q] if outputs else []) + [v, lengths, b]
    wide = len(args) - 2
    shapes = [jax.ShapeDtypeStruct((heads // 2, 128, 256), BF)] if states else []
    if outputs:
        shapes += [
            jax.ShapeDtypeStruct((rows, width), BF),
            jax.ShapeDtypeStruct((rows, width), F32),
        ]
    return pl.pallas_call(
        functools.partial(kda_kernel, ndocs, flip, states, outputs),
        in_specs=[FAR] * len(args),
        out_specs=[WHOLE] * len(shapes),
        out_shape=shapes,
        scratch_shapes=[pltpu.VMEM((rows, width), BF)] * wide
        + [
            pltpu.VMEM(b.shape, F32),
            pltpu.SMEM(lengths.shape, jnp.int32),
            pltpu.SemaphoreType.DMA((wide,)),
            pltpu.SemaphoreType.DMA((2,)),
        ],
        compiler_params=pltpu.CompilerParams(vmem_limit_bytes=limit),
        cost_estimate=CHEAP,
        name="kda_slab",
    )(*args)


def pair_kernel(own_ref, got_ref, pm_ref, pu_ref):
    place = lax.axis_index("ctx")

    def go(first_ref, second_ref):
        for h in range(own_ref.shape[0]):
            z = mm(second_ref[h, :, :128], first_ref[h])
            pm_ref[h] = z[:, :128].astype(BF)
            pu_ref[h] = (z[:, 128:] + second_ref[h, :, 128:].astype(F32)).astype(BF)

    @pl.when(place % 2 == 0)
    def _():
        go(own_ref, got_ref)

    @pl.when(place % 2 == 1)
    def _():
        go(got_ref, own_ref)


def arrived(place, a_ref, b_ref, h):
    x = jnp.where((place // 2) % 2 == 1, a_ref[h].astype(F32), b_ref[h].astype(F32))
    return jnp.where(place < 2, 0.0, x).astype(BF)


def step_kernel(pm_ref, pu_ref, a_ref, b_ref, out_ref):
    place = lax.axis_index("ctx")
    for h in range(pm_ref.shape[0]):
        x = arrived(place, a_ref, b_ref, h)
        out_ref[h] = (mm(pm_ref[h], x) + pu_ref[h].astype(F32)).astype(BF)


def split_kernel(own_ref, got_ref, a_ref, b_ref, mine_ref, send_ref):
    place = lax.axis_index("ctx")

    def go(mu_ref, plain_ref, moved_ref):
        for h in range(own_ref.shape[0]):
            x = arrived(place, a_ref, b_ref, h)
            plain_ref[h] = x
            moved_ref[h] = (mm(mu_ref[h, :, :128], x) + mu_ref[h, :, 128:].astype(F32)).astype(BF)

    @pl.when(place % 2 == 0)
    def _():
        go(own_ref, mine_ref, send_ref)

    @pl.when(place % 2 == 1)
    def _():
        go(got_ref, send_ref, mine_ref)


def whole_call(kernel, name, args, outs):
    return pl.pallas_call(
        kernel,
        in_specs=[WHOLE] * len(args),
        out_specs=[WHOLE] * len(outs),
        out_shape=[jax.ShapeDtypeStruct(o, BF) for o in outs],
        cost_estimate=CHEAP,
        compiler_params=pltpu.CompilerParams(vmem_limit_bytes=VMEM // 2),
        name=name,
    )(*args)


def final_kernel(flip, qe_ref, lo_ref, s_ref, *rest):
    out_ref, held_ref, sem = rest[-3:]
    width = qe_ref.shape[1]
    side = (lax.axis_index("ctx") + flip) % 2
    start = pl.multiple_of(side * width, width)
    parts = 2
    part = width // parts
    copies = []
    for h in range(s_ref.shape[0]):
        cols = slice(h * 128, (h + 1) * 128)
        held_ref[:, cols] = (lo_ref[:, cols] + mm(qe_ref[:, cols], s_ref[h])).astype(BF)
        if (h + 1) * 128 % part == 0:
            i = len(copies)
            copies.append(
                pltpu.make_async_copy(
                    held_ref.at[:, pl.ds(i * part, part)],
                    out_ref.at[:, pl.ds(start + i * part, part)],
                    sem.at[i],
                )
            )
            copies[-1].start()
    for copy in copies:
        copy.wait()


def final(flip, qe, lo, s, heads, previous):
    rows, width = qe.shape
    args, specs, aliases = [qe, lo, s], [WHOLE] * 3, {}
    if previous is not None:
        args.append(previous)
        specs.append(FAR)
        aliases = {3: 0}
    return pl.pallas_call(
        functools.partial(final_kernel, flip),
        in_specs=specs,
        out_specs=FAR,
        out_shape=jax.ShapeDtypeStruct((rows, heads * 128), BF),
        scratch_shapes=[pltpu.VMEM((rows, width), BF), pltpu.SemaphoreType.DMA((2,))],
        input_output_aliases=aliases,
        cost_estimate=CHEAP,
        compiler_params=pltpu.CompilerParams(vmem_limit_bytes=VMEM // 2),
        name="kda_out",
    )(*args)


def window_rows(place, reach, rows, own_ref, mate_ref, out_ref):
    for column in range(2):

        @pl.when(place % 2 == column)
        def _():
            for w in range(reach + 1):
                back = reach // 2 - (w + column) // 2
                if (w + column) % 2 == column:
                    block = own_ref[back]
                else:
                    block = mate_ref[back - 1 + column]
                at = slice(w * rows, (w + 1) * rows)
                out_ref[at, :LATENT] = block[:LATENT].T
                out_ref[at, LATENT:] = block[LATENT:].T


def pick_kernel(own_ref, *refs):
    out_ref, send_ref = refs[-2:]
    place = lax.axis_index("ctx")
    rounds = send_ref.shape[0]
    out_ref[0] = own_ref[...]
    for back in range(rounds):
        for kind in range(2):

            @pl.when((place // 2) % 2 == 1 - kind)
            def _():
                out_ref[back + 1] = refs[2 * back + kind][...]

    for column in range(2):

        @pl.when(place % 2 == column)
        def _():
            send_ref[...] = out_ref[column : column + rounds]


def mask_kernel(ndocs, lengths, bias_ref):
    rows, keys = bias_ref.shape
    place = lax.axis_index("ctx")
    here = place * rows + lax.broadcasted_iota(jnp.int32, (rows, 1), 0)
    there = (place + 1) * rows - keys + lax.broadcasted_iota(jnp.int32, (1, keys), 1)
    doc_q = doc_of(here, lengths, ndocs)
    doc_k = doc_of(there, lengths, ndocs)
    bias_ref[...] = jnp.where((there <= here) & (doc_q == doc_k), 0.0, NEG)


def mask(lengths, rows, keys):
    return pl.pallas_call(
        functools.partial(mask_kernel, lengths.shape[0]),
        in_specs=[SCALARS],
        out_specs=WHOLE,
        out_shape=jax.ShapeDtypeStruct((rows, keys), F32),
        cost_estimate=CHEAP,
        compiler_params=pltpu.CompilerParams(vmem_limit_bytes=VMEM // 2),
        name="window_mask",
    )(lengths)


def mla_kernel(reach, fresh, first, bias_ref, q_ref, ku_ref, vu_ref, *refs):
    out_ref, held_ref, sem = refs[-3:]
    rows = q_ref.shape[0]
    if not fresh:
        lat_ref = refs[0]
    else:
        lat_ref = refs[2]
        window_rows(lax.axis_index("ctx"), reach, rows, *refs[:2], lat_ref)

    factor = math.log2(math.e) / math.sqrt(NOPE + ROPE)
    lat = lat_ref[:, :LATENT]
    rope = lat_ref[:, LATENT:]
    width = held_ref.shape[1]
    part = slice(first * 128, first * 128 + width)
    kn = mm(lat, ku_ref[:, part]).astype(BF)
    vals = mm(lat, vu_ref[:, part]).astype(BF)
    bias = bias_ref[...]
    hs = range(width // 128)
    cols = [slice(h * 128, (h + 1) * 128) for h in hs]
    wide = NOPE + ROPE
    s = [
        mm_nt(
            q_ref[:, (first + h) * wide : (first + h + 1) * wide],
            jnp.concatenate([kn[:, cols[h]], rope], axis=1),
        )
        for h in hs
    ]
    s = [x * factor + bias for x in s]
    w = [jnp.exp2(x - jnp.max(x, axis=1, keepdims=True)) for x in s]
    for h in hs:
        total = jnp.sum(w[h], axis=1, keepdims=True)
        held_ref[:, cols[h]] = (mm(w[h].astype(BF), vals[:, cols[h]]) / total).astype(BF)
    copy = pltpu.make_async_copy(held_ref, out_ref.at[:, part], sem)
    copy.start()
    copy.wait()


def mla(bias, q, ku, vu, blocks, previous, reach, first, count):
    rows = q.shape[0]
    heads = ku.shape[1] // NOPE
    keys = (reach + 1) * rows
    args = [bias, q, ku, vu, *blocks]
    specs = [WHOLE] * len(args)
    out = jax.ShapeDtypeStruct((rows, heads * 128), BF)
    aliases = {}
    if previous is not None:
        aliases = {len(args): 0}
        args.append(previous)
        specs.append(FAR)
    return pl.pallas_call(
        functools.partial(
            mla_kernel,
            reach,
            previous is None,
            first,
        ),
        in_specs=specs,
        out_specs=[WHOLE, FAR] if previous is None else FAR,
        out_shape=[jax.ShapeDtypeStruct((keys, LATENT + ROPE), BF), out]
        if previous is None
        else out,
        scratch_shapes=[
            pltpu.VMEM((rows, count * 128), BF),
            pltpu.SemaphoreType.DMA,
        ],
        input_output_aliases=aliases,
        compiler_params=pltpu.CompilerParams(vmem_limit_bytes=VMEM),
        cost_estimate=CHEAP,
        name="mla_heads",
    )(*args)


def routes(n):
    mate = [i ^ 1 for i in range(n)]
    up = [i ^ 2 for i in range(n)]
    middle = {}
    for pair in range(1, n // 2 - 1, 2):
        for c in range(2):
            middle[2 * pair + c], middle[2 * pair + 2 + c] = 2 * pair + 2 + c, 2 * pair + c
    return mate, up, middle


def swap(x, table):
    n, m = lax.axis_size("ctx"), lax.axis_size("batch")
    if isinstance(table, list):
        return lax.ppermute(x, "ctx", list(enumerate(table)))
    pairs = []
    for i in range(n):
        for j in range(m):
            pairs.append((i * m + j, table[i] * m + j if i in table else i * m + (j ^ 1)))
    return lax.ppermute(x, ("ctx", "batch"), pairs)


def local(
    kda_query,
    kda_key,
    kda_value,
    log_decay,
    write_rate,
    mla_query,
    latents,
    key_up,
    value_up,
    doc_lengths,
):
    n = lax.axis_size("ctx")
    heads = write_rate.shape[1]
    reach = n // 2
    rounds = -(-n // 4)
    mate, up, middle = routes(n)
    kda_args = (doc_lengths, kda_query, kda_key, kda_value, log_decay, write_rate.T)

    lat = latents.T
    shape = (heads // 2, 128, 128)
    def after(x, *others):
        return lax.optimization_barrier((x, others))[0]

    (mu_away,) = kda_half(1, *kda_args, outputs=False, limit=ALL_VMEM)
    mu_got = swap(mu_away, mate)
    args = after(kda_args, mu_away)
    early = after(lat, mu_away)
    moved = [(swap(early, up), swap(early, middle))]
    mu_own, qe_own, lo_own = kda_half(0, *args)
    moved[0] = after(moved[0], mu_own)
    args = after(args, mu_own, moved[0])
    qe_away, lo_away = kda_half(1, *args, states=False)
    for _ in range(rounds - 1):
        a, b = moved[-1]
        moved.append((swap(b, up), swap(a, middle)))
    bias = mask(after(doc_lengths, qe_away), latents.shape[0], (reach + 1) * latents.shape[0])
    lat_own, lat_send = whole_call(
        pick_kernel,
        "pick_latents",
        [after(lat, qe_away), *[x for ab in moved for x in ab]],
        [(rounds + 1, *lat.shape), (rounds, *lat.shape)],
    )
    lat_mate = swap(lat_send, mate)
    mu_got = after(mu_got, bias, lat_own)
    pm, pu = whole_call(pair_kernel, "pair_join", [mu_own, mu_got], [shape, shape])

    def attend(latent_blocks, previous, first, count):
        return mla(
            bias,
            mla_query,
            key_up,
            value_up,
            latent_blocks,
            previous,
            reach,
            first,
            count,
        )

    state = pu
    for step in range(rounds):
        a, b = swap(state, up), swap(state, middle)
        if step < rounds - 1:
            (state,) = whole_call(step_kernel, "pair_step", [pm, pu, a, b], [shape])
    lat_own, _ = lax.optimization_barrier((lat_own, state))
    window, mla_out = attend([lat_own, lat_mate], None, 0, heads // 2)
    a, b, window = lax.optimization_barrier((a, b, window))
    s_own, s_send = whole_call(split_kernel, "slab_states", [mu_own, mu_got, a, b], [shape, shape])
    s_got = swap(s_send, mate)
    window, _ = lax.optimization_barrier((window, s_send))
    mla_out = attend([window], mla_out, heads // 2, heads // 2)
    out = final(0, qe_own, lo_own, s_own, heads, None)
    s_got, mla_out = lax.optimization_barrier((s_got, mla_out))
    kda_out = final(1, qe_away, lo_away, s_got, heads, out)
    return (kda_out, mla_out)


def solution(mesh):
    in_specs = (
        P(("batch", "ctx"), None),
        P(("batch", "ctx"), None),
        P(("batch", "ctx"), None),
        P(("batch", "ctx"), None),
        P(("batch", "ctx"), None),
        P(("batch", "ctx"), None),
        P(("batch", "ctx"), None),
        P(),
        P(),
        P("batch"),
    )
    out_specs = (P(("batch", "ctx"), None), P(("batch", "ctx"), None))
    return jax.shard_map(local, mesh=mesh, in_specs=in_specs, out_specs=out_specs, check_vma=False)
```

```python
import functools
import math

import jax
import jax.numpy as jnp
import numpy as np
from jax import lax
from jax.experimental import pallas as pl
from jax.experimental.pallas import tpu as pltpu
from jax.sharding import PartitionSpec as P

NOPE = 128
ROPE = 64
LATENT = 512
VMEM = 20 * 1024 * 1024
ALL_VMEM = 20 * 1024 * 1024
WHOLE = pl.BlockSpec(memory_space=pltpu.VMEM)
SCALARS = pl.BlockSpec(memory_space=pltpu.SMEM)
FAR = pl.BlockSpec(memory_space=pltpu.HBM)
CHEAP = pl.CostEstimate(flops=0, bytes_accessed=0, transcendentals=0)
BF = jnp.bfloat16
F32 = jnp.float32
NEG = -1e30


def mm(a, b):
    return jnp.dot(a, b, preferred_element_type=F32)


def mm_nt(a, b):
    return lax.dot_general(a, b, (((1,), (1,)), ((), ())), preferred_element_type=F32)


def mm_tn(a, b):
    return lax.dot_general(a, b, (((0,), (0,)), ((), ())), preferred_element_type=F32)


def doc_of(places, lengths_ref, ndocs):
    total = jnp.full(jnp.shape(places), -1, jnp.int32)
    start = 0
    for j in range(ndocs):
        total = total + (start <= places).astype(jnp.int32)
        start = start + lengths_ref[j]
    return total


def kda_kernel(ndocs, flip, fetch, states, outputs, *refs):
    place = lax.axis_index("ctx")
    side = (place + flip) % 2
    later = []
    if fetch:
        far, far_lengths, far_b = refs[:4], refs[4], refs[5]
        held, other, b_ref, refs = refs[6:10], refs[10:14], refs[14], refs[15:]
        lengths, sems = refs[-2:]
        rows, width = held[0].shape

        def copies(blocks, which, first):
            start = pl.multiple_of(which * width, width)
            return [
                pltpu.make_async_copy(source.at[:, pl.ds(start, width)], to, sems.at[first + j])
                for j, (source, to) in enumerate(zip(far, blocks))
            ]

        now = copies(held, side, 0)
        small = [
            pltpu.make_async_copy(far_lengths, lengths, sems.at[8]),
            pltpu.make_async_copy(far_b, b_ref, sems.at[9]),
        ]
        later = copies(other, 1 - side, 4)
        if not outputs:
            later, now = [now[3], *later], now[:3]
        for copy in [*now, *small, *later]:
            copy.start()
    else:
        held, lengths, b_ref, refs = refs[:4], refs[4], refs[5], refs[6:]
        rows, width = held[0].shape
        now, small = [], []
    sc = lengths
    block = dict(zip("gkvq", held))
    if states:
        mu_ref, refs = refs[0], refs[1:]
    if outputs:
        qe_ref, lo_ref = refs[:2]
    half = rows // 2
    heads = width // 128
    base = side * heads
    first = place * rows
    ri = lax.broadcasted_iota(jnp.int32, (rows, rows), 0)
    ci = lax.broadcasted_iota(jnp.int32, (rows, rows), 1)
    tri = (ri >= ci).astype(BF)
    low = ci < half
    eye = (ri == ci).astype(F32)
    zeros = jnp.zeros((half, 128), BF)
    for copy in now[:2]:
        copy.wait()
    cum_all = mm(tri, block["g"][...])

    def halves(top, bottom):
        return jnp.concatenate(
            [jnp.broadcast_to(top, (half, 128)), jnp.broadcast_to(bottom, (half, 128))], axis=0
        )

    hs = range(heads)
    kept, lhs, km, lhs_off, km_off = [], [], [], [], []
    for h in hs:
        cols = slice(h * 128, (h + 1) * 128)
        k = block["k"][:, cols].astype(F32)
        kn = k * lax.rsqrt(jnp.sum(k * k, axis=1, keepdims=True) + 1e-06)
        cum = cum_all[:, cols]
        quarter = half // 2
        m0 = cum[quarter - 1 : quarter]
        m1 = cum[half + quarter - 1 : half + quarter]
        mid = cum[half - 1 : half]
        end = cum[rows - 1 : rows]
        about = cum - halves(m0, m1)
        dp = jnp.exp(about)
        kd = kn * dp
        ku = kn * jnp.exp(-about)
        late = jnp.exp(m1 - mid)
        grow = halves(jnp.exp(m0 * 0.5), jnp.exp(m1 * 0.5))
        wane = halves(jnp.exp((end - m0) * 0.5), jnp.exp((end - m1) * 0.5))
        left, left_off = [kd.astype(BF)], [(kd[half:] * late).astype(BF)]
        queried = None
        if outputs:
            q = block["q"][:, cols].astype(F32)
            qd = q * lax.rsqrt(jnp.sum(q * q, axis=1, keepdims=True) + 1e-06) * dp
            left.append(qd.astype(BF))
            left_off.append((qd[half:] * late).astype(BF))
            queried = qd * grow * grow
        lhs.append(jnp.concatenate(left, axis=0))
        lhs_off.append(jnp.concatenate(left_off, axis=0))
        km.append(ku.astype(BF))
        km_off.append(
            jnp.concatenate([(ku[:half] * jnp.exp(mid - m0)).astype(BF), zeros], axis=0)
        )
        kept.append((kd * grow * grow, ku * wane * wane, queried, jnp.exp(end)))

    for copy in [*now[2:], *small]:
        copy.wait()
    doc_r = doc_of(first + ri, sc, ndocs)
    doc_c = doc_of(first + ci, sc, ndocs)
    prev = doc_of(first - 1, sc, ndocs)
    last = doc_of(first + rows - 1, sc, ndocs)
    same = doc_r == doc_c
    strict = same & (ri > ci)
    causal = same & (ri >= ci)
    follow = (doc_r == prev).astype(F32)
    tail = (doc_r == last).astype(F32)
    keep = (last == prev).astype(F32)
    a, mix, rhs = [], [], []
    for h in hs:
        p = mm_nt(lhs[h], km[h])
        o = mm_nt(lhs_off[h], km_off[h])
        b = jnp.sum(eye * b_ref[pl.ds(base + h, 1), :], axis=1, keepdims=True)
        pa = jnp.concatenate([p[:half], jnp.where(low[half:], o[:half], p[half:rows])], axis=0)
        a.append(jnp.where(strict, pa * b, 0.0))
        if outputs:
            pq = p[rows:]
            pq = jnp.concatenate([pq[:half], jnp.where(low[half:], o[half:], pq[half:])], axis=0)
            mix.append(jnp.where(causal, pq, 0.0).astype(BF))
        v = block["v"][:, h * 128 : (h + 1) * 128].astype(F32)
        rhs.append(
            jnp.concatenate([(kept[h][0] * (b * follow)).astype(BF), (v * b).astype(BF)], axis=1)
        )

    t = [(eye - jnp.where((ri >> 1) == (ci >> 1), a[h], 0.0)).astype(BF) for h in hs]
    a = [a[h].astype(BF) for h in hs]
    bits, low_bit = rows.bit_length() - 1, 1
    while low_bit < bits:
        up_bit = min(low_bit + 3, bits)
        rest = ((ri >> up_bit) == (ci >> up_bit)) & ((ri >> low_bit) != (ci >> low_bit))
        rest = rest.astype(BF)
        w = [mm(a[h] * rest, t[h]).astype(BF) for h in hs]
        left = t
        for step in range(up_bit - low_bit):
            if step + 1 < up_bit - low_bit:
                z = [mm(jnp.concatenate([left[h], w[h]], axis=0), w[h]) for h in hs]
                w = [z[h][rows:].astype(BF) for h in hs]
                z = [z[h][:rows] for h in hs]
            else:
                z = [mm(left[h], w[h]) for h in hs]
            t = [t[h] - z[h] if step == 0 else t[h] + z[h] for h in hs]
            left = [t[h].astype(BF) for h in hs]
        t = left
        low_bit = up_bit

    wu = [mm(t[h], rhs[h]).astype(BF) for h in hs]
    for h in hs:
        cols = slice(h * 128, (h + 1) * 128)
        if states:
            z = mm_tn((kept[h][1] * tail).astype(BF), wu[h])
            mu_ref[h, :, :128] = (eye * (kept[h][3] * keep) - z[:, :128]).astype(BF)
            mu_ref[h, :, 128:] = z[:, 128:].astype(BF)
        if outputs:
            y = mm(mix[h], wu[h])
            qe_ref[:, cols] = (kept[h][2] * follow - y[:, :128]).astype(BF)
            lo_ref[:, cols] = y[:, 128:]
    for copy in later:
        copy.wait()


def kda_call(kernel, in_specs, shapes, scratch, limit, args):
    return pl.pallas_call(
        kernel,
        in_specs=in_specs,
        out_specs=[WHOLE] * len(shapes),
        out_shape=shapes,
        scratch_shapes=scratch,
        cost_estimate=CHEAP,
        compiler_params=pltpu.CompilerParams(vmem_limit_bytes=limit),
        name="kda_slab",
    )(*args)


def kda_first(lengths, q, k, v, g, b):
    rows, width, heads = q.shape[0], q.shape[1] // 2, b.shape[0]
    block = jax.ShapeDtypeStruct((rows, width), BF)
    outs = kda_call(
        functools.partial(kda_kernel, lengths.shape[0], 1, True, True, False),
        [FAR] * 6,
        [block] * 8
        + [
            jax.ShapeDtypeStruct(b.shape, F32),
            jax.ShapeDtypeStruct((heads // 2, 128, 256), BF),
        ],
        [pltpu.SMEM(lengths.shape, jnp.int32), pltpu.SemaphoreType.DMA((10,))],
        ALL_VMEM,
        [pltpu.with_memory_space_constraint(x, pltpu.HBM) for x in (g, k, v, q, lengths, b)],
    )
    return outs[9], outs[:4], outs[4:8], outs[8]


def kda_half(flip, blocks, lengths, b, states):
    rows, width = blocks[0].shape
    shapes = [jax.ShapeDtypeStruct((b.shape[0] // 2, 128, 256), BF)] if states else []
    shapes += [jax.ShapeDtypeStruct((rows, width), BF), jax.ShapeDtypeStruct((rows, width), F32)]
    return kda_call(
        functools.partial(kda_kernel, lengths.shape[0], flip, False, states, True),
        [WHOLE] * 4 + [SCALARS, WHOLE],
        shapes,
        [],
        VMEM,
        [*blocks, lengths, b],
    )


def pair_kernel(own_ref, got_ref, pm_ref, pu_ref):
    place = lax.axis_index("ctx")

    def go(first_ref, second_ref):
        for h in range(own_ref.shape[0]):
            z = mm(second_ref[h, :, :128], first_ref[h])
            pm_ref[h] = z[:, :128].astype(BF)
            pu_ref[h] = (z[:, 128:] + second_ref[h, :, 128:].astype(F32)).astype(BF)

    @pl.when(place % 2 == 0)
    def _():
        go(own_ref, got_ref)

    @pl.when(place % 2 == 1)
    def _():
        go(got_ref, own_ref)


def arrived(place, a_ref, b_ref, h):
    x = jnp.where((place // 2) % 2 == 1, a_ref[h].astype(F32), b_ref[h].astype(F32))
    return jnp.where(place < 2, 0.0, x).astype(BF)


def step_kernel(pm_ref, pu_ref, a_ref, b_ref, out_ref):
    place = lax.axis_index("ctx")
    for h in range(pm_ref.shape[0]):
        x = arrived(place, a_ref, b_ref, h)
        out_ref[h] = (mm(pm_ref[h], x) + pu_ref[h].astype(F32)).astype(BF)


def split_kernel(own_ref, got_ref, a_ref, b_ref, mine_ref, send_ref):
    place = lax.axis_index("ctx")

    def go(mu_ref, plain_ref, moved_ref):
        for h in range(own_ref.shape[0]):
            x = arrived(place, a_ref, b_ref, h)
            plain_ref[h] = x
            moved_ref[h] = (mm(mu_ref[h, :, :128], x) + mu_ref[h, :, 128:].astype(F32)).astype(BF)

    @pl.when(place % 2 == 0)
    def _():
        go(own_ref, mine_ref, send_ref)

    @pl.when(place % 2 == 1)
    def _():
        go(got_ref, send_ref, mine_ref)


def whole_call(kernel, name, args, outs):
    return pl.pallas_call(
        kernel,
        in_specs=[WHOLE] * len(args),
        out_specs=[WHOLE] * len(outs),
        out_shape=[jax.ShapeDtypeStruct(o, BF) for o in outs],
        cost_estimate=CHEAP,
        compiler_params=pltpu.CompilerParams(vmem_limit_bytes=VMEM // 2),
        name=name,
    )(*args)


def final_kernel(flip, qe_ref, lo_ref, s_ref, *rest):
    out_ref, held_ref, sem = rest[-3:]
    width = qe_ref.shape[1]
    side = (lax.axis_index("ctx") + flip) % 2
    start = pl.multiple_of(side * width, width)
    parts = 2
    part = width // parts
    copies = []
    for h in range(s_ref.shape[0]):
        cols = slice(h * 128, (h + 1) * 128)
        held_ref[:, cols] = (lo_ref[:, cols] + mm(qe_ref[:, cols], s_ref[h])).astype(BF)
        if (h + 1) * 128 % part == 0:
            i = len(copies)
            copies.append(
                pltpu.make_async_copy(
                    held_ref.at[:, pl.ds(i * part, part)],
                    out_ref.at[:, pl.ds(start + i * part, part)],
                    sem.at[i],
                )
            )
            copies[-1].start()
    for copy in copies:
        copy.wait()


def final(flip, qe, lo, s, heads, previous):
    rows, width = qe.shape
    args, specs, aliases = [qe, lo, s], [WHOLE] * 3, {}
    if previous is not None:
        args.append(previous)
        specs.append(FAR)
        aliases = {3: 0}
    return pl.pallas_call(
        functools.partial(final_kernel, flip),
        in_specs=specs,
        out_specs=FAR,
        out_shape=jax.ShapeDtypeStruct((rows, heads * 128), BF),
        scratch_shapes=[pltpu.VMEM((rows, width), BF), pltpu.SemaphoreType.DMA((2,))],
        input_output_aliases=aliases,
        cost_estimate=CHEAP,
        compiler_params=pltpu.CompilerParams(vmem_limit_bytes=VMEM // 2),
        name="kda_out",
    )(*args)


def window_rows(place, reach, rows, own_ref, mate_ref, out_ref):
    for column in range(2):

        @pl.when(place % 2 == column)
        def _():
            for w in range(reach + 1):
                back = reach // 2 - (w + column) // 2
                if (w + column) % 2 == column:
                    block = own_ref[back]
                else:
                    block = mate_ref[back - 1 + column]
                at = slice(w * rows, (w + 1) * rows)
                out_ref[at, :LATENT] = block[:LATENT].T
                out_ref[at, LATENT:] = block[LATENT:].T


def pick_kernel(own_ref, *refs):
    out_ref, send_ref = refs[-2:]
    place = lax.axis_index("ctx")
    rounds = send_ref.shape[0]
    out_ref[0] = own_ref[...]
    for back in range(rounds):
        for kind in range(2):

            @pl.when((place // 2) % 2 == 1 - kind)
            def _():
                out_ref[back + 1] = refs[2 * back + kind][...]

    for column in range(2):

        @pl.when(place % 2 == column)
        def _():
            send_ref[...] = out_ref[column : column + rounds]


def mask_kernel(ndocs, lengths, bias_ref):
    rows, keys = bias_ref.shape
    place = lax.axis_index("ctx")
    here = place * rows + lax.broadcasted_iota(jnp.int32, (rows, 1), 0)
    there = (place + 1) * rows - keys + lax.broadcasted_iota(jnp.int32, (1, keys), 1)
    doc_q = doc_of(here, lengths, ndocs)
    doc_k = doc_of(there, lengths, ndocs)
    bias_ref[...] = jnp.where((there <= here) & (doc_q == doc_k), 0.0, NEG)


def mask(lengths, rows, keys):
    return pl.pallas_call(
        functools.partial(mask_kernel, lengths.shape[0]),
        in_specs=[SCALARS],
        out_specs=WHOLE,
        out_shape=jax.ShapeDtypeStruct((rows, keys), F32),
        cost_estimate=CHEAP,
        compiler_params=pltpu.CompilerParams(vmem_limit_bytes=VMEM // 2),
        name="window_mask",
    )(lengths)


def mla_kernel(reach, fresh, first, bias_ref, q_ref, ku_ref, vu_ref, *refs):
    out_ref, held_ref, sem = refs[-3:]
    rows = q_ref.shape[0]
    if not fresh:
        lat_ref = refs[0]
    else:
        lat_ref = refs[2]
        window_rows(lax.axis_index("ctx"), reach, rows, *refs[:2], lat_ref)

    factor = math.log2(math.e) / math.sqrt(NOPE + ROPE)
    lat = lat_ref[:, :LATENT]
    rope = lat_ref[:, LATENT:]
    width = held_ref.shape[1]
    part = slice(first * 128, first * 128 + width)
    kn = mm(lat, ku_ref[:, part]).astype(BF)
    vals = mm(lat, vu_ref[:, part]).astype(BF)
    bias = bias_ref[...]
    hs = range(width // 128)
    cols = [slice(h * 128, (h + 1) * 128) for h in hs]
    wide = NOPE + ROPE
    s = [
        mm_nt(
            q_ref[:, (first + h) * wide : (first + h + 1) * wide],
            jnp.concatenate([kn[:, cols[h]], rope], axis=1),
        )
        for h in hs
    ]
    s = [x * factor + bias for x in s]
    w = [jnp.exp2(x - jnp.max(x, axis=1, keepdims=True)) for x in s]
    for h in hs:
        total = jnp.sum(w[h], axis=1, keepdims=True)
        held_ref[:, cols[h]] = (mm(w[h].astype(BF), vals[:, cols[h]]) / total).astype(BF)
    copy = pltpu.make_async_copy(held_ref, out_ref.at[:, part], sem)
    copy.start()
    copy.wait()


def mla(bias, q, ku, vu, blocks, previous, reach, first, count):
    rows = q.shape[0]
    heads = ku.shape[1] // NOPE
    keys = (reach + 1) * rows
    args = [bias, q, ku, vu, *blocks]
    specs = [WHOLE] * len(args)
    out = jax.ShapeDtypeStruct((rows, heads * 128), BF)
    aliases = {}
    if previous is not None:
        aliases = {len(args): 0}
        args.append(previous)
        specs.append(FAR)
    return pl.pallas_call(
        functools.partial(
            mla_kernel,
            reach,
            previous is None,
            first,
        ),
        in_specs=specs,
        out_specs=[WHOLE, FAR] if previous is None else FAR,
        out_shape=[jax.ShapeDtypeStruct((keys, LATENT + ROPE), BF), out]
        if previous is None
        else out,
        scratch_shapes=[
            pltpu.VMEM((rows, count * 128), BF),
            pltpu.SemaphoreType.DMA,
        ],
        input_output_aliases=aliases,
        compiler_params=pltpu.CompilerParams(vmem_limit_bytes=VMEM),
        cost_estimate=CHEAP,
        name="mla_heads",
    )(*args)


def routes(n):
    mate = [i ^ 1 for i in range(n)]
    up = [i ^ 2 for i in range(n)]
    middle = {}
    for pair in range(1, n // 2 - 1, 2):
        for c in range(2):
            middle[2 * pair + c], middle[2 * pair + 2 + c] = 2 * pair + 2 + c, 2 * pair + c
    return mate, up, middle


def swap(x, table):
    n, m = lax.axis_size("ctx"), lax.axis_size("batch")
    if isinstance(table, list):
        return lax.ppermute(x, "ctx", list(enumerate(table)))
    pairs = []
    for i in range(n):
        for j in range(m):
            pairs.append((i * m + j, table[i] * m + j if i in table else i * m + (j ^ 1)))
    return lax.ppermute(x, ("ctx", "batch"), pairs)


def local(
    kda_query,
    kda_key,
    kda_value,
    log_decay,
    write_rate,
    mla_query,
    latents,
    key_up,
    value_up,
    doc_lengths,
):
    n = lax.axis_size("ctx")
    heads = write_rate.shape[1]
    reach = n // 2
    rounds = -(-n // 4)
    mate, up, middle = routes(n)
    lat = latents.T
    shape = (heads // 2, 128, 128)
    def after(x, *others):
        return lax.optimization_barrier((x, others))[0]

    mu_away, away, own, rates = kda_first(
        doc_lengths, kda_query, kda_key, kda_value, log_decay, write_rate.T
    )
    mu_got = swap(mu_away, mate)
    early = after(lat, mu_away)
    moved = [(swap(early, up), swap(early, middle))]
    mu_own, qe_own, lo_own = kda_half(0, own, doc_lengths, rates, True)
    moved[0] = after(moved[0], mu_own)
    away = after(away, mu_own, moved[0])
    qe_away, lo_away = kda_half(1, away, doc_lengths, rates, False)
    for _ in range(rounds - 1):
        a, b = moved[-1]
        moved.append((swap(b, up), swap(a, middle)))
    bias = mask(after(doc_lengths, qe_away), latents.shape[0], (reach + 1) * latents.shape[0])
    lat_own, lat_send = whole_call(
        pick_kernel,
        "pick_latents",
        [after(lat, qe_away), *[x for ab in moved for x in ab]],
        [(rounds + 1, *lat.shape), (rounds, *lat.shape)],
    )
    lat_mate = swap(lat_send, mate)
    mu_got = after(mu_got, bias, lat_own)
    pm, pu = whole_call(pair_kernel, "pair_join", [mu_own, mu_got], [shape, shape])

    def attend(latent_blocks, previous, first, count):
        return mla(
            bias,
            mla_query,
            key_up,
            value_up,
            latent_blocks,
            previous,
            reach,
            first,
            count,
        )

    state = pu
    for step in range(rounds):
        a, b = swap(state, up), swap(state, middle)
        if step < rounds - 1:
            (state,) = whole_call(step_kernel, "pair_step", [pm, pu, a, b], [shape])
    lat_own, _ = lax.optimization_barrier((lat_own, state))
    window, mla_out = attend([lat_own, lat_mate], None, 0, heads // 2)
    a, b, window = lax.optimization_barrier((a, b, window))
    s_own, s_send = whole_call(split_kernel, "slab_states", [mu_own, mu_got, a, b], [shape, shape])
    s_got = swap(s_send, mate)
    window, _ = lax.optimization_barrier((window, s_send))
    mla_out = attend([window], mla_out, heads // 2, heads // 2)
    out = final(0, qe_own, lo_own, s_own, heads, None)
    s_got, mla_out = lax.optimization_barrier((s_got, mla_out))
    kda_out = final(1, qe_away, lo_away, s_got, heads, out)
    return (kda_out, mla_out)


def solution(mesh):
    in_specs = (
        P(("batch", "ctx"), None),
        P(("batch", "ctx"), None),
        P(("batch", "ctx"), None),
        P(("batch", "ctx"), None),
        P(("batch", "ctx"), None),
        P(("batch", "ctx"), None),
        P(("batch", "ctx"), None),
        P(),
        P(),
        P("batch"),
    )
    out_specs = (P(("batch", "ctx"), None), P(("batch", "ctx"), None))
    return jax.shard_map(local, mesh=mesh, in_specs=in_specs, out_specs=out_specs, check_vma=False)
```

```python
import functools
import math

import jax
import jax.numpy as jnp
import numpy as np
from jax import lax
from jax.experimental import pallas as pl
from jax.experimental.pallas import tpu as pltpu
from jax.sharding import PartitionSpec as P

NOPE = 128
ROPE = 64
LATENT = 512
VMEM = 20 * 1024 * 1024
ALL_VMEM = 20 * 1024 * 1024
WHOLE = pl.BlockSpec(memory_space=pltpu.VMEM)
SCALARS = pl.BlockSpec(memory_space=pltpu.SMEM)
FAR = pl.BlockSpec(memory_space=pltpu.HBM)
CHEAP = pl.CostEstimate(flops=0, bytes_accessed=0, transcendentals=0)
BF = jnp.bfloat16
F32 = jnp.float32
NEG = -1e30


def mm(a, b):
    return jnp.dot(a, b, preferred_element_type=F32)


def mm_nt(a, b):
    return lax.dot_general(a, b, (((1,), (1,)), ((), ())), preferred_element_type=F32)


def mm_tn(a, b):
    return lax.dot_general(a, b, (((0,), (0,)), ((), ())), preferred_element_type=F32)


def doc_of(places, lengths_ref, ndocs):
    total = jnp.full(jnp.shape(places), -1, jnp.int32)
    start = 0
    for j in range(ndocs):
        total = total + (start <= places).astype(jnp.int32)
        start = start + lengths_ref[j]
    return total


def kda_kernel(ndocs, flip, fetch, states, outputs, *refs):
    place = lax.axis_index("ctx")
    side = (place + flip) % 2
    later = []
    if fetch:
        far, far_lengths, far_b = refs[:4], refs[4], refs[5]
        held, other, b_ref, refs = refs[6:10], refs[10:14], refs[14], refs[15:]
        lengths, sems = refs[-2:]
        rows, width = held[0].shape

        def copies(blocks, which, first):
            start = pl.multiple_of(which * width, width)
            return [
                pltpu.make_async_copy(source.at[:, pl.ds(start, width)], to, sems.at[first + j])
                for j, (source, to) in enumerate(zip(far, blocks))
            ]

        now = copies(held, side, 0)
        small = [
            pltpu.make_async_copy(far_lengths, lengths, sems.at[8]),
            pltpu.make_async_copy(far_b, b_ref, sems.at[9]),
        ]
        later = copies(other, 1 - side, 4)
        if not outputs:
            later, now = [now[3], *later], now[:3]
        for copy in [*now, *small, *later]:
            copy.start()
    else:
        held, lengths, b_ref, refs = refs[:4], refs[4], refs[5], refs[6:]
        rows, width = held[0].shape
        now, small = [], []
    sc = lengths
    block = dict(zip("gkvq", held))
    if states:
        mu_ref, refs = refs[0], refs[1:]
    if outputs:
        qe_ref, lo_ref = refs[:2]
    half = rows // 2
    heads = width // 128
    base = side * heads
    first = place * rows
    ri = lax.broadcasted_iota(jnp.int32, (rows, rows), 0)
    ci = lax.broadcasted_iota(jnp.int32, (rows, rows), 1)
    tri = (ri >= ci).astype(BF)
    low = ci < half
    eye = (ri == ci).astype(F32)
    zeros = jnp.zeros((half, 128), BF)
    for copy in now[:2]:
        copy.wait()
    cum_all = mm(tri, block["g"][...])

    def halves(top, bottom):
        return jnp.concatenate(
            [jnp.broadcast_to(top, (half, 128)), jnp.broadcast_to(bottom, (half, 128))], axis=0
        )

    hs = range(heads)
    kept, lhs, km, lhs_off, km_off = [], [], [], [], []
    for h in hs:
        cols = slice(h * 128, (h + 1) * 128)
        k = block["k"][:, cols].astype(F32)
        kn = k * lax.rsqrt(jnp.sum(k * k, axis=1, keepdims=True) + 1e-06)
        cum = cum_all[:, cols]
        quarter = half // 2
        m0 = cum[quarter - 1 : quarter]
        m1 = cum[half + quarter - 1 : half + quarter]
        mid = cum[half - 1 : half]
        end = cum[rows - 1 : rows]
        about = cum - halves(m0, m1)
        dp = jnp.exp(about)
        kd = kn * dp
        ku = kn * jnp.exp(-about)
        late = jnp.exp(m1 - mid)
        grow = halves(jnp.exp(m0 * 0.5), jnp.exp(m1 * 0.5))
        wane = halves(jnp.exp((end - m0) * 0.5), jnp.exp((end - m1) * 0.5))
        left, left_off = [kd.astype(BF)], [(kd[half:] * late).astype(BF)]
        queried = None
        if outputs:
            q = block["q"][:, cols].astype(F32)
            qd = q * lax.rsqrt(jnp.sum(q * q, axis=1, keepdims=True) + 1e-06) * dp
            left.append(qd.astype(BF))
            left_off.append((qd[half:] * late).astype(BF))
            queried = qd * grow * grow
        lhs.append(jnp.concatenate(left, axis=0))
        lhs_off.append(jnp.concatenate(left_off, axis=0))
        km.append(ku.astype(BF))
        km_off.append(
            jnp.concatenate([(ku[:half] * jnp.exp(mid - m0)).astype(BF), zeros], axis=0)
        )
        kept.append((kd * grow * grow, ku * wane * wane, queried, jnp.exp(end)))

    for copy in [*now[2:], *small]:
        copy.wait()
    doc_r = doc_of(first + ri, sc, ndocs)
    doc_c = doc_of(first + ci, sc, ndocs)
    prev = doc_of(first - 1, sc, ndocs)
    last = doc_of(first + rows - 1, sc, ndocs)
    same = doc_r == doc_c
    strict = same & (ri > ci)
    causal = same & (ri >= ci)
    follow = (doc_r == prev).astype(F32)
    tail = (doc_r == last).astype(F32)
    keep = (last == prev).astype(F32)
    a, mix, rhs = [], [], []
    for h in hs:
        p = mm_nt(lhs[h], km[h])
        o = mm_nt(lhs_off[h], km_off[h])
        b = jnp.sum(eye * b_ref[pl.ds(base + h, 1), :], axis=1, keepdims=True)
        pa = jnp.concatenate([p[:half], jnp.where(low[half:], o[:half], p[half:rows])], axis=0)
        a.append(jnp.where(strict, pa * b, 0.0))
        if outputs:
            pq = p[rows:]
            pq = jnp.concatenate([pq[:half], jnp.where(low[half:], o[half:], pq[half:])], axis=0)
            mix.append(jnp.where(causal, pq, 0.0).astype(BF))
        v = block["v"][:, h * 128 : (h + 1) * 128].astype(F32)
        rhs.append(
            jnp.concatenate([(kept[h][0] * (b * follow)).astype(BF), (v * b).astype(BF)], axis=1)
        )

    t = [(eye - jnp.where((ri >> 1) == (ci >> 1), a[h], 0.0)).astype(BF) for h in hs]
    a = [a[h].astype(BF) for h in hs]
    bits, low_bit = rows.bit_length() - 1, 1
    while low_bit < bits:
        up_bit = min(low_bit + 3, bits)
        rest = ((ri >> up_bit) == (ci >> up_bit)) & ((ri >> low_bit) != (ci >> low_bit))
        rest = rest.astype(BF)
        w = [mm(a[h] * rest, t[h]).astype(BF) for h in hs]
        left = t
        for step in range(up_bit - low_bit):
            if step + 1 < up_bit - low_bit:
                z = [mm(jnp.concatenate([left[h], w[h]], axis=0), w[h]) for h in hs]
                w = [z[h][rows:].astype(BF) for h in hs]
                z = [z[h][:rows] for h in hs]
            else:
                z = [mm(left[h], w[h]) for h in hs]
            t = [t[h] - z[h] if step == 0 else t[h] + z[h] for h in hs]
            left = [t[h].astype(BF) for h in hs]
        t = left
        low_bit = up_bit

    wu = [mm(t[h], rhs[h]).astype(BF) for h in hs]
    for h in hs:
        cols = slice(h * 128, (h + 1) * 128)
        if states:
            z = mm_tn((kept[h][1] * tail).astype(BF), wu[h])
            mu_ref[h, :, :128] = (eye * (kept[h][3] * keep) - z[:, :128]).astype(BF)
            mu_ref[h, :, 128:] = z[:, 128:].astype(BF)
        if outputs:
            y = mm(mix[h], wu[h])
            qe_ref[:, cols] = (kept[h][2] * follow - y[:, :128]).astype(BF)
            lo_ref[:, cols] = y[:, 128:]
    for copy in later:
        copy.wait()


def kda_call(kernel, in_specs, shapes, scratch, limit, args):
    return pl.pallas_call(
        kernel,
        in_specs=in_specs,
        out_specs=[WHOLE] * len(shapes),
        out_shape=shapes,
        scratch_shapes=scratch,
        cost_estimate=CHEAP,
        compiler_params=pltpu.CompilerParams(vmem_limit_bytes=limit),
        name="kda_slab",
    )(*args)


def kda_first(lengths, q, k, v, g, b):
    rows, width, heads = q.shape[0], q.shape[1] // 2, b.shape[0]
    block = jax.ShapeDtypeStruct((rows, width), BF)
    outs = kda_call(
        functools.partial(kda_kernel, lengths.shape[0], 1, True, True, False),
        [FAR] * 6,
        [block] * 8
        + [
            jax.ShapeDtypeStruct(b.shape, F32),
            jax.ShapeDtypeStruct((heads // 2, 128, 256), BF),
        ],
        [pltpu.SMEM(lengths.shape, jnp.int32), pltpu.SemaphoreType.DMA((10,))],
        ALL_VMEM,
        [pltpu.with_memory_space_constraint(x, pltpu.HBM) for x in (g, k, v, q, lengths, b)],
    )
    return outs[9], outs[:4], outs[4:8], outs[8]


def kda_half(flip, blocks, lengths, b, states):
    rows, width = blocks[0].shape
    shapes = [jax.ShapeDtypeStruct((b.shape[0] // 2, 128, 256), BF)] if states else []
    shapes += [jax.ShapeDtypeStruct((rows, width), BF), jax.ShapeDtypeStruct((rows, width), F32)]
    return kda_call(
        functools.partial(kda_kernel, lengths.shape[0], flip, False, states, True),
        [WHOLE] * 4 + [SCALARS, WHOLE],
        shapes,
        [],
        VMEM,
        [*blocks, lengths, b],
    )


def pair_kernel(own_ref, got_ref, pm_ref, pu_ref):
    place = lax.axis_index("ctx")

    def go(first_ref, second_ref):
        for h in range(own_ref.shape[0]):
            z = mm(second_ref[h, :, :128], first_ref[h])
            pm_ref[h] = z[:, :128].astype(BF)
            pu_ref[h] = (z[:, 128:] + second_ref[h, :, 128:].astype(F32)).astype(BF)

    @pl.when(place % 2 == 0)
    def _():
        go(own_ref, got_ref)

    @pl.when(place % 2 == 1)
    def _():
        go(got_ref, own_ref)


def arrived(place, a_ref, b_ref, h):
    x = jnp.where((place // 2) % 2 == 1, a_ref[h].astype(F32), b_ref[h].astype(F32))
    return jnp.where(place < 2, 0.0, x).astype(BF)


def step_kernel(pm_ref, pu_ref, a_ref, b_ref, out_ref):
    place = lax.axis_index("ctx")
    for h in range(pm_ref.shape[0]):
        x = arrived(place, a_ref, b_ref, h)
        out_ref[h] = (mm(pm_ref[h], x) + pu_ref[h].astype(F32)).astype(BF)


def split_kernel(own_ref, got_ref, a_ref, b_ref, mine_ref, send_ref):
    place = lax.axis_index("ctx")

    def go(mu_ref, plain_ref, moved_ref):
        for h in range(own_ref.shape[0]):
            x = arrived(place, a_ref, b_ref, h)
            plain_ref[h] = x
            moved_ref[h] = (mm(mu_ref[h, :, :128], x) + mu_ref[h, :, 128:].astype(F32)).astype(BF)

    @pl.when(place % 2 == 0)
    def _():
        go(own_ref, mine_ref, send_ref)

    @pl.when(place % 2 == 1)
    def _():
        go(got_ref, send_ref, mine_ref)


def whole_call(kernel, name, args, outs):
    return pl.pallas_call(
        kernel,
        in_specs=[WHOLE] * len(args),
        out_specs=[WHOLE] * len(outs),
        out_shape=[jax.ShapeDtypeStruct(o, BF) for o in outs],
        cost_estimate=CHEAP,
        compiler_params=pltpu.CompilerParams(vmem_limit_bytes=VMEM // 2),
        name=name,
    )(*args)


def final_kernel(qe_ref, lo_ref, s_ref, *refs):
    held_ref, copies = refs[0], []
    width = qe_ref.shape[1]
    if len(refs) > 1:
        own_ref, out_ref, held_ref, sems = refs
        side = lax.axis_index("ctx") % 2

        def copy_out(source, which, sem):
            start = pl.multiple_of(which * width, width)
            copies.append(
                pltpu.make_async_copy(source, out_ref.at[:, pl.ds(start, width)], sems.at[sem])
            )
            copies[-1].start()

        copy_out(own_ref, side, 0)
    for h in range(s_ref.shape[0]):
        cols = slice(h * 128, (h + 1) * 128)
        held_ref[:, cols] = (lo_ref[:, cols] + mm(qe_ref[:, cols], s_ref[h])).astype(BF)
    if len(refs) > 1:
        copy_out(held_ref, 1 - side, 1)
    for copy in copies:
        copy.wait()


def final(qe, lo, s, own=None):
    rows, width = qe.shape
    args = [qe, lo, s] + ([] if own is None else [own])
    scratch = [] if own is None else [pltpu.VMEM((rows, width), BF), pltpu.SemaphoreType.DMA((2,))]
    return pl.pallas_call(
        final_kernel,
        in_specs=[WHOLE] * len(args),
        out_specs=WHOLE if own is None else FAR,
        out_shape=jax.ShapeDtypeStruct((rows, width if own is None else 2 * width), BF),
        scratch_shapes=scratch,
        cost_estimate=CHEAP,
        compiler_params=pltpu.CompilerParams(vmem_limit_bytes=VMEM // 2),
        name="kda_out",
    )(*args)


def window_rows(place, reach, rows, own_ref, mate_ref, out_ref):
    for column in range(2):

        @pl.when(place % 2 == column)
        def _():
            for w in range(reach + 1):
                back = reach // 2 - (w + column) // 2
                if (w + column) % 2 == column:
                    block = own_ref[back]
                else:
                    block = mate_ref[back - 1 + column]
                at = slice(w * rows, (w + 1) * rows)
                out_ref[at, :LATENT] = block[:LATENT].T
                out_ref[at, LATENT:] = block[LATENT:].T


def pick_kernel(own_ref, *refs):
    out_ref, send_ref = refs[-2:]
    place = lax.axis_index("ctx")
    rounds = send_ref.shape[0]
    out_ref[0] = own_ref[...]
    for back in range(rounds):
        for kind in range(2):

            @pl.when((place // 2) % 2 == 1 - kind)
            def _():
                out_ref[back + 1] = refs[2 * back + kind][...]

    for column in range(2):

        @pl.when(place % 2 == column)
        def _():
            send_ref[...] = out_ref[column : column + rounds]


def mask_kernel(ndocs, lengths, bias_ref):
    rows, keys = bias_ref.shape
    place = lax.axis_index("ctx")
    here = place * rows + lax.broadcasted_iota(jnp.int32, (rows, 1), 0)
    there = (place + 1) * rows - keys + lax.broadcasted_iota(jnp.int32, (1, keys), 1)
    doc_q = doc_of(here, lengths, ndocs)
    doc_k = doc_of(there, lengths, ndocs)
    bias_ref[...] = jnp.where((there <= here) & (doc_q == doc_k), 0.0, NEG)


def mask(lengths, rows, keys):
    return pl.pallas_call(
        functools.partial(mask_kernel, lengths.shape[0]),
        in_specs=[SCALARS],
        out_specs=WHOLE,
        out_shape=jax.ShapeDtypeStruct((rows, keys), F32),
        cost_estimate=CHEAP,
        compiler_params=pltpu.CompilerParams(vmem_limit_bytes=VMEM // 2),
        name="window_mask",
    )(lengths)


def mla_kernel(reach, fresh, first, bias_ref, q_ref, ku_ref, vu_ref, *refs):
    rows = q_ref.shape[0]
    copies = []
    if fresh:
        lat_ref, held_ref = refs[2:]
        window_rows(lax.axis_index("ctx"), reach, rows, *refs[:2], lat_ref)
    else:
        lat_ref, before_ref, out_ref, held_ref, sems = refs
        copies.append(pltpu.make_async_copy(before_ref, out_ref.at[:, : first * 128], sems.at[0]))
        copies[0].start()

    factor = math.log2(math.e) / math.sqrt(NOPE + ROPE)
    lat = lat_ref[:, :LATENT]
    rope = lat_ref[:, LATENT:]
    width = held_ref.shape[1]
    part = slice(first * 128, first * 128 + width)
    kn = mm(lat, ku_ref[:, part]).astype(BF)
    vals = mm(lat, vu_ref[:, part]).astype(BF)
    bias = bias_ref[...]
    hs = range(width // 128)
    cols = [slice(h * 128, (h + 1) * 128) for h in hs]
    wide = NOPE + ROPE
    s = [
        mm_nt(
            q_ref[:, (first + h) * wide : (first + h + 1) * wide],
            jnp.concatenate([kn[:, cols[h]], rope], axis=1),
        )
        for h in hs
    ]
    s = [x * factor + bias for x in s]
    w = [jnp.exp2(x - jnp.max(x, axis=1, keepdims=True)) for x in s]
    for h in hs:
        total = jnp.sum(w[h], axis=1, keepdims=True)
        held_ref[:, cols[h]] = (mm(w[h].astype(BF), vals[:, cols[h]]) / total).astype(BF)
    if not fresh:
        copies.append(pltpu.make_async_copy(held_ref, out_ref.at[:, part], sems.at[1]))
        copies[1].start()
    for copy in copies:
        copy.wait()


def mla(bias, q, ku, vu, blocks, before, reach, first, count):
    rows = q.shape[0]
    keys = (reach + 1) * rows
    fresh = before is None
    args = [bias, q, ku, vu, *blocks] + ([] if fresh else [before])
    if fresh:
        shapes = [(keys, LATENT + ROPE), (rows, count * 128)]
        scratch = []
    else:
        shapes = [(rows, (first + count) * 128)]
        scratch = [pltpu.VMEM((rows, count * 128), BF), pltpu.SemaphoreType.DMA((2,))]
    return pl.pallas_call(
        functools.partial(mla_kernel, reach, fresh, first),
        in_specs=[WHOLE] * len(args),
        out_specs=[WHOLE if fresh else FAR] * len(shapes),
        out_shape=[jax.ShapeDtypeStruct(shape, BF) for shape in shapes],
        scratch_shapes=scratch,
        compiler_params=pltpu.CompilerParams(vmem_limit_bytes=VMEM * max(1, keys // 1024)),
        cost_estimate=CHEAP,
        name="mla_heads",
    )(*args)


def routes(n):
    mate = [i ^ 1 for i in range(n)]
    up = [i ^ 2 for i in range(n)]
    middle = {}
    for pair in range(1, n // 2 - 1, 2):
        for c in range(2):
            middle[2 * pair + c], middle[2 * pair + 2 + c] = 2 * pair + 2 + c, 2 * pair + c
    return mate, up, middle


def swap(x, table):
    n, m = lax.axis_size("ctx"), lax.axis_size("batch")
    if isinstance(table, list):
        return lax.ppermute(x, "ctx", list(enumerate(table)))
    pairs = []
    for i in range(n):
        for j in range(m):
            pairs.append((i * m + j, table[i] * m + j if i in table else i * m + (j ^ 1)))
    return lax.ppermute(x, ("ctx", "batch"), pairs)


def local(
    kda_query,
    kda_key,
    kda_value,
    log_decay,
    write_rate,
    mla_query,
    latents,
    key_up,
    value_up,
    doc_lengths,
):
    n = lax.axis_size("ctx")
    heads = write_rate.shape[1]
    reach = n // 2
    rounds = -(-n // 4)
    mate, up, middle = routes(n)
    lat = latents.T
    shape = (heads // 2, 128, 128)
    def after(x, *others):
        return lax.optimization_barrier((x, others))[0]

    mu_away, away, own, rates = kda_first(
        doc_lengths, kda_query, kda_key, kda_value, log_decay, write_rate.T
    )
    mu_got = swap(mu_away, mate)
    early = after(lat, mu_away)
    moved = [(swap(early, up), swap(early, middle))]
    mu_own, qe_own, lo_own = kda_half(0, own, doc_lengths, rates, True)
    moved[0] = after(moved[0], mu_own)
    away = after(away, mu_own, moved[0])
    qe_away, lo_away = kda_half(1, away, doc_lengths, rates, False)
    for _ in range(rounds - 1):
        a, b = moved[-1]
        moved.append((swap(b, up), swap(a, middle)))
    lat_own, lat_send = whole_call(
        pick_kernel,
        "pick_latents",
        [after(lat, qe_away), *[x for ab in moved for x in ab]],
        [(rounds + 1, *lat.shape), (rounds, *lat.shape)],
    )
    lat_mate = swap(lat_send, mate)
    mu_got = after(mu_got, lat_own)
    pm, pu = whole_call(pair_kernel, "pair_join", [mu_own, mu_got], [shape, shape])
    bias = mask(after(doc_lengths, pm), latents.shape[0], (reach + 1) * latents.shape[0])

    def attend(latent_blocks, previous, first, count):
        return mla(
            bias,
            mla_query,
            key_up,
            value_up,
            latent_blocks,
            previous,
            reach,
            first,
            count,
        )

    state = pu
    for step in range(rounds):
        a, b = after((swap(state, up), swap(state, middle)), bias)
        if step < rounds - 1:
            (state,) = whole_call(step_kernel, "pair_step", [pm, pu, a, b], [shape])
    lat_own, _ = lax.optimization_barrier((lat_own, state))
    early_heads = heads * 3 // 8
    window, mla_out = attend([lat_own, lat_mate], None, 0, early_heads)
    a, b, window = lax.optimization_barrier((a, b, window))
    s_own, s_send = whole_call(split_kernel, "slab_states", [mu_own, mu_got, a, b], [shape, shape])
    s_got = swap(s_send, mate)
    window, _ = lax.optimization_barrier((window, s_send))
    (mla_out,) = attend([window], mla_out, early_heads, heads - early_heads)
    out = final(qe_own, lo_own, s_own)
    s_got, mla_out = lax.optimization_barrier((s_got, mla_out))
    kda_out = final(qe_away, lo_away, s_got, out)
    return (kda_out, mla_out)


def solution(mesh):
    in_specs = (
        P(("batch", "ctx"), None),
        P(("batch", "ctx"), None),
        P(("batch", "ctx"), None),
        P(("batch", "ctx"), None),
        P(("batch", "ctx"), None),
        P(("batch", "ctx"), None),
        P(("batch", "ctx"), None),
        P(),
        P(),
        P("batch"),
    )
    out_specs = (P(("batch", "ctx"), None), P(("batch", "ctx"), None))
    return jax.shard_map(local, mesh=mesh, in_specs=in_specs, out_specs=out_specs, check_vma=False)
```

```python
import functools
import math

import jax
import jax.numpy as jnp
import numpy as np
from jax import lax
from jax.experimental import pallas as pl
from jax.experimental.pallas import tpu as pltpu
from jax.sharding import PartitionSpec as P

NOPE = 128
ROPE = 64
LATENT = 512
VMEM = 20 * 1024 * 1024
ALL_VMEM = 20 * 1024 * 1024
WHOLE = pl.BlockSpec(memory_space=pltpu.VMEM)
SCALARS = pl.BlockSpec(memory_space=pltpu.SMEM)
FAR = pl.BlockSpec(memory_space=pltpu.HBM)
CHEAP = pl.CostEstimate(flops=0, bytes_accessed=0, transcendentals=0)
BF = jnp.bfloat16
F32 = jnp.float32
NEG = -1e30


def mm(a, b):
    return jnp.dot(a, b, preferred_element_type=F32)


def mm_nt(a, b):
    return lax.dot_general(a, b, (((1,), (1,)), ((), ())), preferred_element_type=F32)


def mm_tn(a, b):
    return lax.dot_general(a, b, (((0,), (0,)), ((), ())), preferred_element_type=F32)


def doc_of(places, lengths_ref, ndocs):
    total = jnp.full(jnp.shape(places), -1, jnp.int32)
    start = 0
    for j in range(ndocs):
        total = total + (start <= places).astype(jnp.int32)
        start = start + lengths_ref[j]
    return total


def kda_kernel(ndocs, flip, fetch, states, outputs, *refs):
    place = lax.axis_index("ctx")
    side = (place + flip) % 2
    later = []
    if fetch:
        far, far_lengths, far_b = refs[:4], refs[4], refs[5]
        held, other, b_ref, refs = refs[6:10], refs[10:14], refs[14], refs[15:]
        lengths, sems = refs[-2:]
        rows, width = held[0].shape

        def copies(blocks, which, first):
            start = pl.multiple_of(which * width, width)
            return [
                pltpu.make_async_copy(source.at[:, pl.ds(start, width)], to, sems.at[first + j])
                for j, (source, to) in enumerate(zip(far, blocks))
            ]

        now = copies(held, side, 0)
        small = [
            pltpu.make_async_copy(far_lengths, lengths, sems.at[8]),
            pltpu.make_async_copy(far_b, b_ref, sems.at[9]),
        ]
        later = copies(other, 1 - side, 4)
        if not outputs:
            later, now = [now[3], *later], now[:3]
        for copy in [*now, *small, *later]:
            copy.start()
    else:
        held, lengths, b_ref, refs = refs[:4], refs[4], refs[5], refs[6:]
        rows, width = held[0].shape
        now, small = [], []
    sc = lengths
    block = dict(zip("gkvq", held))
    if states:
        mu_ref, refs = refs[0], refs[1:]
    if outputs:
        qe_ref, lo_ref = refs[:2]
    half = rows // 2
    heads = width // 128
    base = side * heads
    first = place * rows
    ri = lax.broadcasted_iota(jnp.int32, (rows, rows), 0)
    ci = lax.broadcasted_iota(jnp.int32, (rows, rows), 1)
    tri = (ri >= ci).astype(BF)
    low = ci < half
    eye = (ri == ci).astype(F32)
    zeros = jnp.zeros((half, 128), BF)
    for copy in now[:2]:
        copy.wait()
    cum_all = mm(tri, block["g"][...])

    def halves(top, bottom):
        return jnp.concatenate(
            [jnp.broadcast_to(top, (half, 128)), jnp.broadcast_to(bottom, (half, 128))], axis=0
        )

    hs = range(heads)
    kept, lhs, km, lhs_off, km_off = [], [], [], [], []
    for h in hs:
        cols = slice(h * 128, (h + 1) * 128)
        k = block["k"][:, cols].astype(F32)
        kn = k * lax.rsqrt(jnp.sum(k * k, axis=1, keepdims=True) + 1e-06)
        cum = cum_all[:, cols]
        quarter = half // 2
        m0 = cum[quarter - 1 : quarter]
        m1 = cum[half + quarter - 1 : half + quarter]
        mid = cum[half - 1 : half]
        end = cum[rows - 1 : rows]
        about = cum - halves(m0, m1)
        dp = jnp.exp(about)
        kd = kn * dp
        ku = kn * jnp.exp(-about)
        late = jnp.exp(m1 - mid)
        grow = halves(jnp.exp(m0 * 0.5), jnp.exp(m1 * 0.5))
        wane = halves(jnp.exp((end - m0) * 0.5), jnp.exp((end - m1) * 0.5))
        left, left_off = [kd.astype(BF)], [(kd[half:] * late).astype(BF)]
        queried = None
        if outputs:
            q = block["q"][:, cols].astype(F32)
            qd = q * lax.rsqrt(jnp.sum(q * q, axis=1, keepdims=True) + 1e-06) * dp
            left.append(qd.astype(BF))
            left_off.append((qd[half:] * late).astype(BF))
            queried = qd * grow * grow
        lhs.append(jnp.concatenate(left, axis=0))
        lhs_off.append(jnp.concatenate(left_off, axis=0))
        km.append(ku.astype(BF))
        km_off.append(
            jnp.concatenate([(ku[:half] * jnp.exp(mid - m0)).astype(BF), zeros], axis=0)
        )
        kept.append((kd * grow * grow, ku * wane * wane, queried, jnp.exp(end)))

    for copy in [*now[2:], *small]:
        copy.wait()
    doc_r = doc_of(first + ri, sc, ndocs)
    doc_c = doc_of(first + ci, sc, ndocs)
    prev = doc_of(first - 1, sc, ndocs)
    last = doc_of(first + rows - 1, sc, ndocs)
    same = doc_r == doc_c
    strict = same & (ri > ci)
    causal = same & (ri >= ci)
    follow = (doc_r == prev).astype(F32)
    tail = (doc_r == last).astype(F32)
    keep = (last == prev).astype(F32)
    a, mix, rhs = [], [], []
    for h in hs:
        p = mm_nt(lhs[h], km[h])
        o = mm_nt(lhs_off[h], km_off[h])
        b = jnp.sum(eye * b_ref[pl.ds(base + h, 1), :], axis=1, keepdims=True)
        pa = jnp.concatenate([p[:half], jnp.where(low[half:], o[:half], p[half:rows])], axis=0)
        a.append(jnp.where(strict, pa * b, 0.0))
        if outputs:
            pq = p[rows:]
            pq = jnp.concatenate([pq[:half], jnp.where(low[half:], o[half:], pq[half:])], axis=0)
            mix.append(jnp.where(causal, pq, 0.0).astype(BF))
        v = block["v"][:, h * 128 : (h + 1) * 128].astype(F32)
        rhs.append(
            jnp.concatenate([(kept[h][0] * (b * follow)).astype(BF), (v * b).astype(BF)], axis=1)
        )

    t = [(eye - jnp.where((ri >> 1) == (ci >> 1), a[h], 0.0)).astype(BF) for h in hs]
    a = [a[h].astype(BF) for h in hs]
    bits, low_bit = rows.bit_length() - 1, 1
    while low_bit < bits:
        up_bit = min(low_bit + 3, bits)
        rest = ((ri >> up_bit) == (ci >> up_bit)) & ((ri >> low_bit) != (ci >> low_bit))
        rest = rest.astype(BF)
        w = [mm(a[h] * rest, t[h]).astype(BF) for h in hs]
        left = t
        for step in range(up_bit - low_bit):
            if step + 1 < up_bit - low_bit:
                z = [mm(jnp.concatenate([left[h], w[h]], axis=0), w[h]) for h in hs]
                w = [z[h][rows:].astype(BF) for h in hs]
                z = [z[h][:rows] for h in hs]
            else:
                z = [mm(left[h], w[h]) for h in hs]
            t = [t[h] - z[h] if step == 0 else t[h] + z[h] for h in hs]
            left = [t[h].astype(BF) for h in hs]
        t = left
        low_bit = up_bit

    wu = [mm(t[h], rhs[h]).astype(BF) for h in hs]
    for h in hs:
        cols = slice(h * 128, (h + 1) * 128)
        if states:
            z = mm_tn((kept[h][1] * tail).astype(BF), wu[h])
            mu_ref[h, :, :128] = (eye * (kept[h][3] * keep) - z[:, :128]).astype(BF)
            mu_ref[h, :, 128:] = z[:, 128:].astype(BF)
        if outputs:
            y = mm(mix[h], wu[h])
            qe_ref[:, cols] = (kept[h][2] * follow - y[:, :128]).astype(BF)
            lo_ref[:, cols] = y[:, 128:]
    for copy in later:
        copy.wait()


def kda_call(kernel, in_specs, shapes, scratch, limit, args):
    return pl.pallas_call(
        kernel,
        in_specs=in_specs,
        out_specs=[WHOLE] * len(shapes),
        out_shape=shapes,
        scratch_shapes=scratch,
        cost_estimate=CHEAP,
        compiler_params=pltpu.CompilerParams(vmem_limit_bytes=limit),
        name="kda_slab",
    )(*args)


def kda_first(lengths, q, k, v, g, b):
    rows, width, heads = q.shape[0], q.shape[1] // 2, b.shape[0]
    block = jax.ShapeDtypeStruct((rows, width), BF)
    outs = kda_call(
        functools.partial(kda_kernel, lengths.shape[0], 1, True, True, False),
        [FAR] * 6,
        [block] * 8
        + [
            jax.ShapeDtypeStruct(b.shape, F32),
            jax.ShapeDtypeStruct((heads // 2, 128, 256), BF),
        ],
        [pltpu.SMEM(lengths.shape, jnp.int32), pltpu.SemaphoreType.DMA((10,))],
        ALL_VMEM,
        [pltpu.with_memory_space_constraint(x, pltpu.HBM) for x in (g, k, v, q, lengths, b)],
    )
    return outs[9], outs[:4], outs[4:8], outs[8]


def kda_half(flip, blocks, lengths, b, states):
    rows, width = blocks[0].shape
    shapes = [jax.ShapeDtypeStruct((b.shape[0] // 2, 128, 256), BF)] if states else []
    shapes += [jax.ShapeDtypeStruct((rows, width), BF), jax.ShapeDtypeStruct((rows, width), F32)]
    return kda_call(
        functools.partial(kda_kernel, lengths.shape[0], flip, False, states, True),
        [WHOLE] * 4 + [SCALARS, WHOLE],
        shapes,
        [],
        VMEM,
        [*blocks, lengths, b],
    )


def pair_kernel(own_ref, got_ref, pm_ref, pu_ref):
    place = lax.axis_index("ctx")

    def go(first_ref, second_ref):
        for h in range(own_ref.shape[0]):
            z = mm(second_ref[h, :, :128], first_ref[h])
            pm_ref[h] = z[:, :128].astype(BF)
            pu_ref[h] = (z[:, 128:] + second_ref[h, :, 128:].astype(F32)).astype(BF)

    @pl.when(place % 2 == 0)
    def _():
        go(own_ref, got_ref)

    @pl.when(place % 2 == 1)
    def _():
        go(got_ref, own_ref)


def on_arrival(a_ref, b_ref, body):
    pair = lax.axis_index("ctx") // 2

    @pl.when(pair == 0)
    def _():
        body(None)

    @pl.when(pair % 2 == 1)
    def _():
        body(a_ref)

    @pl.when((pair % 2 == 0) & (pair > 0))
    def _():
        body(b_ref)


def step_kernel(pm_ref, pu_ref, a_ref, b_ref, out_ref):
    def body(x_ref):
        for h in range(pm_ref.shape[0]):
            if x_ref is None:
                out_ref[h] = pu_ref[h]
            else:
                out_ref[h] = (mm(pm_ref[h], x_ref[h]) + pu_ref[h].astype(F32)).astype(BF)

    on_arrival(a_ref, b_ref, body)


def split_kernel(own_ref, got_ref, a_ref, b_ref, mine_ref, send_ref):
    def go(x_ref, mu_ref, plain_ref, moved_ref):
        for h in range(own_ref.shape[0]):
            u = mu_ref[h, :, 128:]
            if x_ref is None:
                plain_ref[h] = jnp.zeros_like(u)
                moved_ref[h] = u
            else:
                plain_ref[h] = x_ref[h]
                moved_ref[h] = (mm(mu_ref[h, :, :128], x_ref[h]) + u.astype(F32)).astype(BF)

    def body(x_ref):
        place = lax.axis_index("ctx")

        @pl.when(place % 2 == 0)
        def _():
            go(x_ref, own_ref, mine_ref, send_ref)

        @pl.when(place % 2 == 1)
        def _():
            go(x_ref, got_ref, send_ref, mine_ref)

    on_arrival(a_ref, b_ref, body)


def whole_call(kernel, name, args, outs):
    return pl.pallas_call(
        kernel,
        in_specs=[WHOLE] * len(args),
        out_specs=[WHOLE] * len(outs),
        out_shape=[jax.ShapeDtypeStruct(o, BF) for o in outs],
        cost_estimate=CHEAP,
        compiler_params=pltpu.CompilerParams(vmem_limit_bytes=VMEM // 2),
        name=name,
    )(*args)


def final_kernel(qe_ref, lo_ref, s_ref, *refs):
    held_ref, copies = refs[0], []
    width = qe_ref.shape[1]
    if len(refs) > 1:
        own_ref, out_ref, held_ref, sems = refs
        side = lax.axis_index("ctx") % 2

        def copy_out(source, which, sem):
            start = pl.multiple_of(which * width, width)
            copies.append(
                pltpu.make_async_copy(source, out_ref.at[:, pl.ds(start, width)], sems.at[sem])
            )
            copies[-1].start()

        copy_out(own_ref, side, 0)
    for h in range(s_ref.shape[0]):
        cols = slice(h * 128, (h + 1) * 128)
        held_ref[:, cols] = (lo_ref[:, cols] + mm(qe_ref[:, cols], s_ref[h])).astype(BF)
    if len(refs) > 1:
        copy_out(held_ref, 1 - side, 1)
    for copy in copies:
        copy.wait()


def final(qe, lo, s, own=None):
    rows, width = qe.shape
    args = [qe, lo, s] + ([] if own is None else [own])
    scratch = [] if own is None else [pltpu.VMEM((rows, width), BF), pltpu.SemaphoreType.DMA((2,))]
    return pl.pallas_call(
        final_kernel,
        in_specs=[WHOLE] * len(args),
        out_specs=WHOLE if own is None else FAR,
        out_shape=jax.ShapeDtypeStruct((rows, width if own is None else 2 * width), BF),
        scratch_shapes=scratch,
        cost_estimate=CHEAP,
        compiler_params=pltpu.CompilerParams(vmem_limit_bytes=VMEM // 2),
        name="kda_out",
    )(*args)


def window_rows(place, reach, rows, own_ref, mate_ref, out_ref):
    for column in range(2):

        @pl.when(place % 2 == column)
        def _():
            for w in range(reach + 1):
                back = reach // 2 - (w + column) // 2
                if (w + column) % 2 == column:
                    block = own_ref[back]
                else:
                    block = mate_ref[back - 1 + column]
                at = slice(w * rows, (w + 1) * rows)
                out_ref[at, :LATENT] = block[:LATENT].T
                out_ref[at, LATENT:] = block[LATENT:].T


def pick_kernel(own_ref, *refs):
    out_ref, send_ref = refs[-2:]
    place = lax.axis_index("ctx")
    rounds = send_ref.shape[0]
    out_ref[0] = own_ref[...]
    for back in range(rounds):
        for kind in range(2):

            @pl.when((place // 2) % 2 == 1 - kind)
            def _():
                out_ref[back + 1] = refs[2 * back + kind][...]

    for column in range(2):

        @pl.when(place % 2 == column)
        def _():
            send_ref[...] = out_ref[column : column + rounds]


def mask_kernel(ndocs, lengths, bias_ref):
    rows, keys = bias_ref.shape
    place = lax.axis_index("ctx")
    here = place * rows + lax.broadcasted_iota(jnp.int32, (rows, 1), 0)
    there = (place + 1) * rows - keys + lax.broadcasted_iota(jnp.int32, (1, keys), 1)
    doc_q = doc_of(here, lengths, ndocs)
    doc_k = doc_of(there, lengths, ndocs)
    bias_ref[...] = jnp.where((there <= here) & (doc_q == doc_k), 0.0, NEG)


def mask(lengths, rows, keys):
    return pl.pallas_call(
        functools.partial(mask_kernel, lengths.shape[0]),
        in_specs=[SCALARS],
        out_specs=WHOLE,
        out_shape=jax.ShapeDtypeStruct((rows, keys), F32),
        cost_estimate=CHEAP,
        compiler_params=pltpu.CompilerParams(vmem_limit_bytes=VMEM // 2),
        name="window_mask",
    )(lengths)


def mla_kernel(reach, fresh, first, bias_ref, q_ref, ku_ref, vu_ref, *refs):
    rows = q_ref.shape[0]
    copies = []
    if fresh:
        lat_ref, held_ref = refs[2:]
        window_rows(lax.axis_index("ctx"), reach, rows, *refs[:2], lat_ref)
    else:
        lat_ref, before_ref, out_ref, held_ref, sems = refs
        copies.append(pltpu.make_async_copy(before_ref, out_ref.at[:, : first * 128], sems.at[0]))
        copies[0].start()

    factor = math.log2(math.e) / math.sqrt(NOPE + ROPE)
    lat = lat_ref[:, :LATENT]
    rope = lat_ref[:, LATENT:]
    width = held_ref.shape[1]
    part = slice(first * 128, first * 128 + width)
    kn = mm(lat, ku_ref[:, part]).astype(BF)
    vals = mm(lat, vu_ref[:, part]).astype(BF)
    bias = bias_ref[...]
    hs = range(width // 128)
    cols = [slice(h * 128, (h + 1) * 128) for h in hs]
    wide = NOPE + ROPE
    s = [
        mm_nt(
            q_ref[:, (first + h) * wide : (first + h + 1) * wide],
            jnp.concatenate([kn[:, cols[h]], rope], axis=1),
        )
        for h in hs
    ]
    s = [x * factor + bias for x in s]
    w = [jnp.exp2(x - jnp.max(x, axis=1, keepdims=True)) for x in s]
    for h in hs:
        total = jnp.sum(w[h], axis=1, keepdims=True)
        held_ref[:, cols[h]] = (mm(w[h].astype(BF), vals[:, cols[h]]) / total).astype(BF)
    if not fresh:
        copies.append(pltpu.make_async_copy(held_ref, out_ref.at[:, part], sems.at[1]))
        copies[1].start()
    for copy in copies:
        copy.wait()


def mla(bias, q, ku, vu, blocks, before, reach, first, count):
    rows = q.shape[0]
    keys = (reach + 1) * rows
    fresh = before is None
    args = [bias, q, ku, vu, *blocks] + ([] if fresh else [before])
    if fresh:
        shapes = [(keys, LATENT + ROPE), (rows, count * 128)]
        scratch = []
    else:
        shapes = [(rows, (first + count) * 128)]
        scratch = [pltpu.VMEM((rows, count * 128), BF), pltpu.SemaphoreType.DMA((2,))]
    return pl.pallas_call(
        functools.partial(mla_kernel, reach, fresh, first),
        in_specs=[WHOLE] * len(args),
        out_specs=[WHOLE if fresh else FAR] * len(shapes),
        out_shape=[jax.ShapeDtypeStruct(shape, BF) for shape in shapes],
        scratch_shapes=scratch,
        compiler_params=pltpu.CompilerParams(vmem_limit_bytes=VMEM * max(1, keys // 1024)),
        cost_estimate=CHEAP,
        name="mla_heads",
    )(*args)


def routes(n):
    mate = [i ^ 1 for i in range(n)]
    up = [i ^ 2 for i in range(n)]
    middle = {}
    for pair in range(1, n // 2 - 1, 2):
        for c in range(2):
            middle[2 * pair + c], middle[2 * pair + 2 + c] = 2 * pair + 2 + c, 2 * pair + c
    return mate, up, middle


def swap(x, table):
    n, m = lax.axis_size("ctx"), lax.axis_size("batch")
    if isinstance(table, list):
        return lax.ppermute(x, "ctx", list(enumerate(table)))
    pairs = []
    for i in range(n):
        for j in range(m):
            pairs.append((i * m + j, table[i] * m + j if i in table else i * m + (j ^ 1)))
    return lax.ppermute(x, ("ctx", "batch"), pairs)


def local(
    kda_query,
    kda_key,
    kda_value,
    log_decay,
    write_rate,
    mla_query,
    latents,
    key_up,
    value_up,
    doc_lengths,
):
    n = lax.axis_size("ctx")
    heads = write_rate.shape[1]
    reach = n // 2
    rounds = -(-n // 4)
    mate, up, middle = routes(n)
    lat = latents.T
    shape = (heads // 2, 128, 128)
    def after(x, *others):
        return lax.optimization_barrier((x, others))[0]

    mu_away, away, own, rates = kda_first(
        doc_lengths, kda_query, kda_key, kda_value, log_decay, write_rate.T
    )
    mu_got = swap(mu_away, mate)
    early = after(lat, mu_away)
    moved = [(swap(early, up), swap(early, middle))]
    mu_own, qe_own, lo_own = kda_half(0, own, doc_lengths, rates, True)
    moved[0] = after(moved[0], mu_own)
    away = after(away, mu_own, moved[0])
    qe_away, lo_away = kda_half(1, away, doc_lengths, rates, False)
    for _ in range(rounds - 1):
        a, b = moved[-1]
        moved.append((swap(b, up), swap(a, middle)))
    lat_own, lat_send = whole_call(
        pick_kernel,
        "pick_latents",
        [after(lat, qe_away), *[x for ab in moved for x in ab]],
        [(rounds + 1, *lat.shape), (rounds, *lat.shape)],
    )
    lat_mate = swap(lat_send, mate)
    mu_got = after(mu_got, lat_own)
    pm, pu = whole_call(pair_kernel, "pair_join", [mu_own, mu_got], [shape, shape])
    bias = mask(after(doc_lengths, pm), latents.shape[0], (reach + 1) * latents.shape[0])

    def attend(latent_blocks, previous, first, count):
        return mla(
            bias,
            mla_query,
            key_up,
            value_up,
            latent_blocks,
            previous,
            reach,
            first,
            count,
        )

    state = pu
    for step in range(rounds):
        a, b = after((swap(state, up), swap(state, middle)), bias)
        if step < rounds - 1:
            (state,) = whole_call(step_kernel, "pair_step", [pm, pu, a, b], [shape])
    lat_own, _ = lax.optimization_barrier((lat_own, state))
    early_heads = heads * 3 // 8
    window, mla_out = attend([lat_own, lat_mate], None, 0, early_heads)
    a, b, window = lax.optimization_barrier((a, b, window))
    s_own, s_send = whole_call(split_kernel, "slab_states", [mu_own, mu_got, a, b], [shape, shape])
    s_got = swap(s_send, mate)
    window, _ = lax.optimization_barrier((window, s_send))
    (mla_out,) = attend([window], mla_out, early_heads, heads - early_heads)
    out = final(qe_own, lo_own, s_own)
    s_got, mla_out = lax.optimization_barrier((s_got, mla_out))
    kda_out = final(qe_away, lo_away, s_got, out)
    return (kda_out, mla_out)


def solution(mesh):
    in_specs = (
        P(("batch", "ctx"), None),
        P(("batch", "ctx"), None),
        P(("batch", "ctx"), None),
        P(("batch", "ctx"), None),
        P(("batch", "ctx"), None),
        P(("batch", "ctx"), None),
        P(("batch", "ctx"), None),
        P(),
        P(),
        P("batch"),
    )
    out_specs = (P(("batch", "ctx"), None), P(("batch", "ctx"), None))
    return jax.shard_map(local, mesh=mesh, in_specs=in_specs, out_specs=out_specs, check_vma=False)
```

```python
import functools
import math

import jax
import jax.numpy as jnp
import numpy as np
from jax import lax
from jax.experimental import pallas as pl
from jax.experimental.pallas import tpu as pltpu
from jax.sharding import PartitionSpec as P

NOPE = 128
ROPE = 64
LATENT = 512
VMEM = 20 * 1024 * 1024
ALL_VMEM = 20 * 1024 * 1024
WHOLE = pl.BlockSpec(memory_space=pltpu.VMEM)
SCALARS = pl.BlockSpec(memory_space=pltpu.SMEM)
FAR = pl.BlockSpec(memory_space=pltpu.HBM)
CHEAP = pl.CostEstimate(flops=0, bytes_accessed=0, transcendentals=0)
BF = jnp.bfloat16
F32 = jnp.float32
NEG = -1e30


def mm(a, b):
    return jnp.dot(a, b, preferred_element_type=F32)


def mm_nt(a, b):
    return lax.dot_general(a, b, (((1,), (1,)), ((), ())), preferred_element_type=F32)


def mm_tn(a, b):
    return lax.dot_general(a, b, (((0,), (0,)), ((), ())), preferred_element_type=F32)


def doc_of(places, lengths_ref, ndocs):
    total = jnp.full(jnp.shape(places), -1, jnp.int32)
    start = 0
    for j in range(ndocs):
        total = total + (start <= places).astype(jnp.int32)
        start = start + lengths_ref[j]
    return total


def kda_kernel(ndocs, flip, fetch, states, outputs, *refs):
    place = lax.axis_index("ctx")
    side = (place + flip) % 2
    later = []
    if fetch:
        far, far_lengths, far_b = refs[:4], refs[4], refs[5]
        held, other, b_ref, refs = refs[6:10], refs[10:14], refs[14], refs[15:]
        lengths, sems = refs[-2:]
        rows, width = held[0].shape

        def copies(blocks, which, first):
            start = pl.multiple_of(which * width, width)
            return [
                pltpu.make_async_copy(source.at[:, pl.ds(start, width)], to, sems.at[first + j])
                for j, (source, to) in enumerate(zip(far, blocks))
            ]

        now = copies(held, side, 0)
        small = [
            pltpu.make_async_copy(far_lengths, lengths, sems.at[8]),
            pltpu.make_async_copy(far_b, b_ref, sems.at[9]),
        ]
        later = copies(other, 1 - side, 4)
        if not outputs:
            later, now = [now[3], *later], now[:3]
        for copy in [*now, *small, *later]:
            copy.start()
    else:
        held, lengths, b_ref, refs = refs[:4], refs[4], refs[5], refs[6:]
        rows, width = held[0].shape
        now, small = [], []
    sc = lengths
    block = dict(zip("gkvq", held))
    if states:
        mu_ref, refs = refs[0], refs[1:]
    if outputs:
        qe_ref, lo_ref = refs[:2]
    half = rows // 2
    heads = width // 128
    base = side * heads
    first = place * rows
    ri = lax.broadcasted_iota(jnp.int32, (rows, rows), 0)
    ci = lax.broadcasted_iota(jnp.int32, (rows, rows), 1)
    tri = (ri >= ci).astype(BF)
    low = ci < half
    eye = (ri == ci).astype(F32)
    zeros = jnp.zeros((half, 128), BF)
    for copy in now[:2]:
        copy.wait()
    cum_all = mm(tri, block["g"][...])

    def halves(top, bottom):
        return jnp.concatenate(
            [jnp.broadcast_to(top, (half, 128)), jnp.broadcast_to(bottom, (half, 128))], axis=0
        )

    hs = range(heads)
    kept, lhs, km, lhs_off, km_off = [], [], [], [], []
    for h in hs:
        cols = slice(h * 128, (h + 1) * 128)
        k = block["k"][:, cols].astype(F32)
        kn = k * lax.rsqrt(jnp.sum(k * k, axis=1, keepdims=True) + 1e-06)
        cum = cum_all[:, cols]
        quarter = half // 2
        m0 = cum[quarter - 1 : quarter]
        m1 = cum[half + quarter - 1 : half + quarter]
        mid = cum[half - 1 : half]
        end = cum[rows - 1 : rows]
        about = cum - halves(m0, m1)
        dp = jnp.exp(about)
        kd = kn * dp
        ku = kn * jnp.exp(-about)
        late = jnp.exp(m1 - mid)
        grow = halves(jnp.exp(m0 * 0.5), jnp.exp(m1 * 0.5))
        wane = halves(jnp.exp((end - m0) * 0.5), jnp.exp((end - m1) * 0.5))
        left, left_off = [kd.astype(BF)], [(kd[half:] * late).astype(BF)]
        queried = None
        if outputs:
            q = block["q"][:, cols].astype(F32)
            qd = q * lax.rsqrt(jnp.sum(q * q, axis=1, keepdims=True) + 1e-06) * dp
            left.append(qd.astype(BF))
            left_off.append((qd[half:] * late).astype(BF))
            queried = qd * grow * grow
        lhs.append(jnp.concatenate(left, axis=0))
        lhs_off.append(jnp.concatenate(left_off, axis=0))
        km.append(ku.astype(BF))
        km_off.append(
            jnp.concatenate([(ku[:half] * jnp.exp(mid - m0)).astype(BF), zeros], axis=0)
        )
        kept.append((kd * grow * grow, ku * wane * wane, queried, jnp.exp(end)))

    for copy in [*now[2:], *small]:
        copy.wait()
    doc_r = doc_of(first + ri, sc, ndocs)
    doc_c = doc_of(first + ci, sc, ndocs)
    prev = doc_of(first - 1, sc, ndocs)
    last = doc_of(first + rows - 1, sc, ndocs)
    same = doc_r == doc_c
    strict = same & (ri > ci)
    causal = same & (ri >= ci)
    follow = (doc_r == prev).astype(F32)
    tail = (doc_r == last).astype(F32)
    keep = (last == prev).astype(F32)
    a, mix, rhs = [], [], []
    for h in hs:
        p = mm_nt(lhs[h], km[h])
        o = mm_nt(lhs_off[h], km_off[h])
        b = jnp.sum(eye * b_ref[pl.ds(base + h, 1), :], axis=1, keepdims=True)
        pa = jnp.concatenate([p[:half], jnp.where(low[half:], o[:half], p[half:rows])], axis=0)
        a.append(jnp.where(strict, pa * b, 0.0))
        if outputs:
            pq = p[rows:]
            pq = jnp.concatenate([pq[:half], jnp.where(low[half:], o[half:], pq[half:])], axis=0)
            mix.append(jnp.where(causal, pq, 0.0).astype(BF))
        v = block["v"][:, h * 128 : (h + 1) * 128].astype(F32)
        rhs.append(
            jnp.concatenate([(kept[h][0] * (b * follow)).astype(BF), (v * b).astype(BF)], axis=1)
        )

    t = [(eye - jnp.where((ri >> 1) == (ci >> 1), a[h], 0.0)).astype(BF) for h in hs]
    a = [a[h].astype(BF) for h in hs]
    bits, low_bit = rows.bit_length() - 1, 1
    while low_bit < bits:
        up_bit = min(low_bit + 3, bits)
        rest = ((ri >> up_bit) == (ci >> up_bit)) & ((ri >> low_bit) != (ci >> low_bit))
        rest = rest.astype(BF)
        w = [mm(a[h] * rest, t[h]).astype(BF) for h in hs]
        left = t
        for step in range(up_bit - low_bit):
            if step + 1 < up_bit - low_bit:
                z = [mm(jnp.concatenate([left[h], w[h]], axis=0), w[h]) for h in hs]
                w = [z[h][rows:].astype(BF) for h in hs]
                z = [z[h][:rows] for h in hs]
            else:
                z = [mm(left[h], w[h]) for h in hs]
            t = [t[h] - z[h] if step == 0 else t[h] + z[h] for h in hs]
            left = [t[h].astype(BF) for h in hs]
        t = left
        low_bit = up_bit

    wu = [mm(t[h], rhs[h]).astype(BF) for h in hs]
    for h in hs:
        cols = slice(h * 128, (h + 1) * 128)
        if states:
            z = mm_tn((kept[h][1] * tail).astype(BF), wu[h])
            mu_ref[h, :, :128] = (eye * (kept[h][3] * keep) - z[:, :128]).astype(BF)
            mu_ref[h, :, 128:] = z[:, 128:].astype(BF)
        if outputs:
            y = mm(mix[h], wu[h])
            qe_ref[:, cols] = (kept[h][2] * follow - y[:, :128]).astype(BF)
            lo_ref[:, cols] = y[:, 128:]
    for copy in later:
        copy.wait()


def kda_call(kernel, in_specs, shapes, scratch, limit, args):
    return pl.pallas_call(
        kernel,
        in_specs=in_specs,
        out_specs=[WHOLE] * len(shapes),
        out_shape=shapes,
        scratch_shapes=scratch,
        cost_estimate=CHEAP,
        compiler_params=pltpu.CompilerParams(vmem_limit_bytes=limit),
        name="kda_slab",
    )(*args)


def kda_first(lengths, q, k, v, g, b):
    rows, width, heads = q.shape[0], q.shape[1] // 2, b.shape[0]
    block = jax.ShapeDtypeStruct((rows, width), BF)
    outs = kda_call(
        functools.partial(kda_kernel, lengths.shape[0], 1, True, True, False),
        [FAR] * 6,
        [block] * 8
        + [
            jax.ShapeDtypeStruct(b.shape, F32),
            jax.ShapeDtypeStruct((heads // 2, 128, 256), BF),
        ],
        [pltpu.SMEM(lengths.shape, jnp.int32), pltpu.SemaphoreType.DMA((10,))],
        ALL_VMEM,
        [pltpu.with_memory_space_constraint(x, pltpu.HBM) for x in (g, k, v, q, lengths, b)],
    )
    return outs[9], outs[:4], outs[4:8], outs[8]


def kda_half(flip, blocks, lengths, b, states):
    rows, width = blocks[0].shape
    shapes = [jax.ShapeDtypeStruct((b.shape[0] // 2, 128, 256), BF)] if states else []
    shapes += [jax.ShapeDtypeStruct((rows, width), BF), jax.ShapeDtypeStruct((rows, width), F32)]
    return kda_call(
        functools.partial(kda_kernel, lengths.shape[0], flip, False, states, True),
        [WHOLE] * 4 + [SCALARS, WHOLE],
        shapes,
        [],
        VMEM,
        [*blocks, lengths, b],
    )


def pair_kernel(own_ref, got_ref, pm_ref, pu_ref):
    place = lax.axis_index("ctx")

    def go(first_ref, second_ref):
        for h in range(own_ref.shape[0]):
            z = mm(second_ref[h, :, :128], first_ref[h])
            pm_ref[h] = z[:, :128].astype(BF)
            pu_ref[h] = (z[:, 128:] + second_ref[h, :, 128:].astype(F32)).astype(BF)

    @pl.when(place % 2 == 0)
    def _():
        go(own_ref, got_ref)

    @pl.when(place % 2 == 1)
    def _():
        go(got_ref, own_ref)


def on_arrival(a_ref, b_ref, body):
    pair = lax.axis_index("ctx") // 2

    @pl.when(pair == 0)
    def _():
        body(None)

    @pl.when(pair % 2 == 1)
    def _():
        body(a_ref)

    @pl.when((pair % 2 == 0) & (pair > 0))
    def _():
        body(b_ref)


def step_kernel(pm_ref, pu_ref, a_ref, b_ref, out_ref):
    def body(x_ref):
        for h in range(pm_ref.shape[0]):
            if x_ref is None:
                out_ref[h] = pu_ref[h]
            else:
                out_ref[h] = (mm(pm_ref[h], x_ref[h]) + pu_ref[h].astype(F32)).astype(BF)

    on_arrival(a_ref, b_ref, body)


def split_kernel(own_ref, got_ref, a_ref, b_ref, mine_ref, send_ref):
    def go(x_ref, mu_ref, plain_ref, moved_ref):
        for h in range(own_ref.shape[0]):
            u = mu_ref[h, :, 128:]
            if x_ref is None:
                plain_ref[h] = jnp.zeros_like(u)
                moved_ref[h] = u
            else:
                plain_ref[h] = x_ref[h]
                moved_ref[h] = (mm(mu_ref[h, :, :128], x_ref[h]) + u.astype(F32)).astype(BF)

    def body(x_ref):
        place = lax.axis_index("ctx")

        @pl.when(place % 2 == 0)
        def _():
            go(x_ref, own_ref, mine_ref, send_ref)

        @pl.when(place % 2 == 1)
        def _():
            go(x_ref, got_ref, send_ref, mine_ref)

    on_arrival(a_ref, b_ref, body)


def whole_call(kernel, name, args, outs):
    return pl.pallas_call(
        kernel,
        in_specs=[WHOLE] * len(args),
        out_specs=[WHOLE] * len(outs),
        out_shape=[jax.ShapeDtypeStruct(o, BF) for o in outs],
        cost_estimate=CHEAP,
        compiler_params=pltpu.CompilerParams(vmem_limit_bytes=VMEM // 2),
        name=name,
    )(*args)


def final_kernel(qe_ref, lo_ref, s_ref, *refs):
    held_ref, copies = refs[0], []
    width = qe_ref.shape[1]
    if len(refs) > 1:
        own_ref, out_ref, held_ref, sems = refs
        side = lax.axis_index("ctx") % 2

        def copy_out(source, which, sem, first, count):
            start = pl.multiple_of(which * width + first, 128)
            copies.append(
                pltpu.make_async_copy(
                    source.at[:, pl.ds(first, count)],
                    out_ref.at[:, pl.ds(start, count)],
                    sems.at[sem],
                )
            )
            copies[-1].start()

        copy_out(own_ref, side, 0, 0, width)
    for h in range(s_ref.shape[0]):
        cols = slice(h * 128, (h + 1) * 128)
        held_ref[:, cols] = (lo_ref[:, cols] + mm(qe_ref[:, cols], s_ref[h])).astype(BF)
        if len(refs) > 1 and (h + 1) % 4 == 0:
            copy_out(held_ref, 1 - side, (h + 1) // 4, h * 128 - 384, 512)
    for copy in copies:
        copy.wait()


def final(qe, lo, s, own=None):
    rows, width = qe.shape
    args = [qe, lo, s] + ([] if own is None else [own])
    scratch = [] if own is None else [pltpu.VMEM((rows, width), BF), pltpu.SemaphoreType.DMA((3,))]
    return pl.pallas_call(
        final_kernel,
        in_specs=[WHOLE] * len(args),
        out_specs=WHOLE if own is None else FAR,
        out_shape=jax.ShapeDtypeStruct((rows, width if own is None else 2 * width), BF),
        scratch_shapes=scratch,
        cost_estimate=CHEAP,
        compiler_params=pltpu.CompilerParams(vmem_limit_bytes=VMEM // 2),
        name="kda_out",
    )(*args)


def window_rows(place, reach, rows, own_ref, mate_ref, out_ref):
    for column in range(2):

        @pl.when(place % 2 == column)
        def _():
            for w in range(reach + 1):
                back = reach // 2 - (w + column) // 2
                if (w + column) % 2 == column:
                    block = own_ref[back]
                else:
                    block = mate_ref[back - 1 + column]
                at = slice(w * rows, (w + 1) * rows)
                out_ref[at, :LATENT] = block[:LATENT].T
                out_ref[at, LATENT:] = block[LATENT:].T


def pick_kernel(own_ref, *refs):
    out_ref, send_ref = refs[-2:]
    place = lax.axis_index("ctx")
    rounds = send_ref.shape[0]
    out_ref[0] = own_ref[...]
    for back in range(rounds):
        for kind in range(2):

            @pl.when((place // 2) % 2 == 1 - kind)
            def _():
                out_ref[back + 1] = refs[2 * back + kind][...]

    for column in range(2):

        @pl.when(place % 2 == column)
        def _():
            send_ref[...] = out_ref[column : column + rounds]


def mask_kernel(ndocs, lengths, bias_ref):
    rows, keys = bias_ref.shape
    place = lax.axis_index("ctx")
    here = place * rows + lax.broadcasted_iota(jnp.int32, (rows, 1), 0)
    there = (place + 1) * rows - keys + lax.broadcasted_iota(jnp.int32, (1, keys), 1)
    doc_q = doc_of(here, lengths, ndocs)
    doc_k = doc_of(there, lengths, ndocs)
    bias_ref[...] = jnp.where((there <= here) & (doc_q == doc_k), 0.0, NEG)


def mask(lengths, rows, keys):
    return pl.pallas_call(
        functools.partial(mask_kernel, lengths.shape[0]),
        in_specs=[SCALARS],
        out_specs=WHOLE,
        out_shape=jax.ShapeDtypeStruct((rows, keys), F32),
        cost_estimate=CHEAP,
        compiler_params=pltpu.CompilerParams(vmem_limit_bytes=VMEM // 2),
        name="window_mask",
    )(lengths)


def mla_kernel(reach, fresh, first, bias_ref, q_ref, ku_ref, vu_ref, *refs):
    rows = q_ref.shape[0]
    copies = []
    if fresh:
        lat_ref, held_ref = refs[2:]
        window_rows(lax.axis_index("ctx"), reach, rows, *refs[:2], lat_ref)
    else:
        lat_ref, before_ref, out_ref, held_ref, sems = refs
        copies.append(pltpu.make_async_copy(before_ref, out_ref.at[:, : first * 128], sems.at[0]))
        copies[0].start()

    factor = math.log2(math.e) / math.sqrt(NOPE + ROPE)
    lat = lat_ref[:, :LATENT]
    rope = lat_ref[:, LATENT:]
    width = held_ref.shape[1]
    part = slice(first * 128, first * 128 + width)
    kn = mm(lat, ku_ref[:, part]).astype(BF)
    vals = mm(lat, vu_ref[:, part]).astype(BF)
    bias = bias_ref[...]
    hs = range(width // 128)
    cols = [slice(h * 128, (h + 1) * 128) for h in hs]
    wide = NOPE + ROPE
    s = [
        mm_nt(
            q_ref[:, (first + h) * wide : (first + h + 1) * wide],
            jnp.concatenate([kn[:, cols[h]], rope], axis=1),
        )
        for h in hs
    ]
    s = [x * factor + bias for x in s]
    w = [jnp.exp2(x - jnp.max(x, axis=1, keepdims=True)) for x in s]
    for h in hs:
        total = jnp.sum(w[h], axis=1, keepdims=True)
        held_ref[:, cols[h]] = (mm(w[h].astype(BF), vals[:, cols[h]]) / total).astype(BF)
    if not fresh:
        copies.append(pltpu.make_async_copy(held_ref, out_ref.at[:, part], sems.at[1]))
        copies[1].start()
    for copy in copies:
        copy.wait()


def mla(bias, q, ku, vu, blocks, before, reach, first, count):
    rows = q.shape[0]
    keys = (reach + 1) * rows
    fresh = before is None
    args = [bias, q, ku, vu, *blocks] + ([] if fresh else [before])
    if fresh:
        shapes = [(keys, LATENT + ROPE), (rows, count * 128)]
        scratch = []
    else:
        shapes = [(rows, (first + count) * 128)]
        scratch = [pltpu.VMEM((rows, count * 128), BF), pltpu.SemaphoreType.DMA((2,))]
    return pl.pallas_call(
        functools.partial(mla_kernel, reach, fresh, first),
        in_specs=[WHOLE] * len(args),
        out_specs=[WHOLE if fresh else FAR] * len(shapes),
        out_shape=[jax.ShapeDtypeStruct(shape, BF) for shape in shapes],
        scratch_shapes=scratch,
        compiler_params=pltpu.CompilerParams(vmem_limit_bytes=VMEM * max(1, keys // 1024)),
        cost_estimate=CHEAP,
        name="mla_heads",
    )(*args)


def routes(n):
    mate = [i ^ 1 for i in range(n)]
    up = [i ^ 2 for i in range(n)]
    middle = {}
    for pair in range(1, n // 2 - 1, 2):
        for c in range(2):
            middle[2 * pair + c], middle[2 * pair + 2 + c] = 2 * pair + 2 + c, 2 * pair + c
    return mate, up, middle


def swap(x, table):
    n, m = lax.axis_size("ctx"), lax.axis_size("batch")
    if isinstance(table, list):
        return lax.ppermute(x, "ctx", list(enumerate(table)))
    pairs = []
    for i in range(n):
        for j in range(m):
            pairs.append((i * m + j, table[i] * m + j if i in table else i * m + (j ^ 1)))
    return lax.ppermute(x, ("ctx", "batch"), pairs)


def local(
    kda_query,
    kda_key,
    kda_value,
    log_decay,
    write_rate,
    mla_query,
    latents,
    key_up,
    value_up,
    doc_lengths,
):
    n = lax.axis_size("ctx")
    heads = write_rate.shape[1]
    reach = n // 2
    rounds = -(-n // 4)
    mate, up, middle = routes(n)
    lat = latents.T
    shape = (heads // 2, 128, 128)
    def after(x, *others):
        return lax.optimization_barrier((x, others))[0]

    mu_away, away, own, rates = kda_first(
        doc_lengths, kda_query, kda_key, kda_value, log_decay, write_rate.T
    )
    mu_got = swap(mu_away, mate)
    early = after(lat, mu_away)
    moved = [(swap(early, up), swap(early, middle))]
    mu_own, qe_own, lo_own = kda_half(0, own, doc_lengths, rates, True)
    moved[0] = after(moved[0], mu_own)
    away = after(away, mu_own, moved[0])
    qe_away, lo_away = kda_half(1, away, doc_lengths, rates, False)
    for _ in range(rounds - 1):
        a, b = moved[-1]
        moved.append((swap(b, up), swap(a, middle)))
    lat_own, lat_send = whole_call(
        pick_kernel,
        "pick_latents",
        [after(lat, qe_away), *[x for ab in moved for x in ab]],
        [(rounds + 1, *lat.shape), (rounds, *lat.shape)],
    )
    lat_mate = swap(lat_send, mate)
    mu_got = after(mu_got, lat_own)
    pm, pu = whole_call(pair_kernel, "pair_join", [mu_own, mu_got], [shape, shape])
    bias = mask(after(doc_lengths, pm), latents.shape[0], (reach + 1) * latents.shape[0])

    def attend(latent_blocks, previous, first, count):
        return mla(
            bias,
            mla_query,
            key_up,
            value_up,
            latent_blocks,
            previous,
            reach,
            first,
            count,
        )

    state = pu
    for step in range(rounds):
        a, b = after((swap(state, up), swap(state, middle)), bias)
        if step < rounds - 1:
            (state,) = whole_call(step_kernel, "pair_step", [pm, pu, a, b], [shape])
    lat_own, _ = lax.optimization_barrier((lat_own, state))
    early_heads = heads * 3 // 8
    window, mla_out = attend([lat_own, lat_mate], None, 0, early_heads)
    a, b, window = lax.optimization_barrier((a, b, window))
    s_own, s_send = whole_call(split_kernel, "slab_states", [mu_own, mu_got, a, b], [shape, shape])
    s_got = swap(s_send, mate)
    window, _ = lax.optimization_barrier((window, s_send))
    (mla_out,) = attend([window], mla_out, early_heads, heads - early_heads)
    out = final(qe_own, lo_own, s_own)
    s_got, mla_out = lax.optimization_barrier((s_got, mla_out))
    kda_out = final(qe_away, lo_away, s_got, out)
    return (kda_out, mla_out)


def solution(mesh):
    in_specs = (
        P(("batch", "ctx"), None),
        P(("batch", "ctx"), None),
        P(("batch", "ctx"), None),
        P(("batch", "ctx"), None),
        P(("batch", "ctx"), None),
        P(("batch", "ctx"), None),
        P(("batch", "ctx"), None),
        P(),
        P(),
        P("batch"),
    )
    out_specs = (P(("batch", "ctx"), None), P(("batch", "ctx"), None))
    return jax.shard_map(local, mesh=mesh, in_specs=in_specs, out_specs=out_specs, check_vma=False)
```
